256 devices in a mesh: dp: 32 (over y, x, core), mp: 8 (over z).
Axes of the slice: x: 4, y: 4, z: 8, core: 2. Of those that a mesh axis runs over, the one named last changes fastest.
Arguments:
- activations: bfloat16 [32768, 2048], P('dp')
- output_grads: bfloat16 [2, 32768, 8192], P(None, 'dp', 'mp')
- token_counts: int32 [32, 4], P('dp'), may hold values from 64 to 256, as said below
- weights: float32 [2, 2048, 8192], P(None, 'dp', 'mp')
- row_state: float32 [2, 2048], P(None, 'dp')
- col_state: float32 [2, 8192], P(None, 'mp')
Outputs:
- update: float32 [2, 2048, 8192], P(None, 'dp', 'mp')
- new_weights: float32 [2, 2048, 8192], P(None, 'dp', 'mp')
- new_rows: float32 [2, 2048], P(None, 'dp')
- new_cols: float32 [2, 8192], P(None, 'mp')
The draws below stay inside these ranges and needn't reach their ends.
Inputs may be any that keep to these rules, and one draw needn't show every extreme that they name: `token_counts`: live counts of micro-batches; groups of higher index hold more live tokens on the whole.
All inputs are finite; a program needn't handle non-finite values.
Results may differ from the reference program's by a relative error of at most 0.0003.
Values sent between devices are 32-bit elements; how exact they have to be, the bound alone decides.
No kernel may reach another device: no remote copies, remote signals or barrier semaphores. Data moves between devices by JAX's collectives and lax.ppermute only.
A program may use at most 128 MiB of HBM per device.

```python
import jax
import jax.numpy as jnp
from jax import lax

D = 2048
FF = 8192
SLOT = 256
MB = 4
GROUPS = 32
TOK_DEV = 1024
TOKENS = 32768


def draw_activations(key, part):
    key = jax.random.fold_in(key, 11)
    k_vals, k_jit = jax.random.split(key, 2)
    column = jnp.arange(D, dtype=jnp.float32) / (D - 1)
    scales = 10.0 ** column * jnp.exp(jax.random.uniform(k_jit, (D,), jnp.float32, -0.35, 0.35))
    values = jax.random.normal(k_vals, (TOKENS, D), jnp.float32)
    return (values * scales[None, :]).astype(jnp.bfloat16)


def draw_output_grads(key, part):
    key = jax.random.fold_in(key, 12)
    k_vals, k_jit = jax.random.split(key, 2)
    column = jnp.arange(FF, dtype=jnp.float32) / (FF - 1)
    scales = 10.0 ** column[None, :] * jnp.exp(jax.random.uniform(k_jit, (2, FF), jnp.float32, -0.35, 0.35))
    values = jax.random.normal(k_vals, (2, TOKENS, FF), jnp.float32)
    return (values * scales[:, None, :]).astype(jnp.bfloat16)


def draw_token_counts(key, part):
    key = jax.random.fold_in(key, 13)
    rows = jnp.arange(GROUPS, dtype=jnp.int32)[:, None]
    base = SLOT // 4 + SLOT // 2 * rows // max(GROUPS - 1, 1)
    extra = jax.random.randint(key, (GROUPS, MB), 0, SLOT // 4 + 1, dtype=jnp.int32)
    counts = base + extra
    counts = counts.at[GROUPS - 1, MB - 1].set(SLOT)
    counts = counts.at[0, 0].set(SLOT // 4)
    return counts


def draw_weights(key, part):
    key = jax.random.fold_in(key, 14)
    rows = jnp.arange(D, dtype=jnp.float32)[:, None] / (D - 1)
    cols = jnp.arange(FF, dtype=jnp.float32)[None, :] / (FF - 1)
    scales = 0.3 * 10.0 ** (0.5 * (rows + cols))
    values = jax.random.normal(key, (2, D, FF), jnp.float32)
    return values * scales[None, :, :]


def expected_total():
    return GROUPS * MB * SLOT * 0.625


def draw_row_state(key, part):
    key = jax.random.fold_in(key, 15)
    level = jnp.exp(jax.random.uniform(key, (2, D), jnp.float32, jnp.log(0.02), jnp.log(0.2)))
    return level * 100.0 * 20.0 / expected_total()


def draw_col_state(key, part):
    key = jax.random.fold_in(key, 16)
    cols = jnp.arange(FF, dtype=jnp.float32) / (FF - 1)
    level = jnp.exp(jax.random.uniform(key, (2, FF), jnp.float32, jnp.log(0.02), jnp.log(0.2)))
    return level * (10.0 ** (2.0 * cols))[None, :] * 20.0 / expected_total()


def setup_inputs(seed: int = 0) -> dict:
    keys = jax.random.split(jax.random.key(seed), 7)
    return {
        "activations": draw_activations(jax.random.fold_in(keys[6], 71), 0),
        "output_grads": draw_output_grads(jax.random.fold_in(keys[6], 71), 0),
        "token_counts": draw_token_counts(jax.random.fold_in(keys[6], 71), 0),
        "weights": draw_weights(jax.random.fold_in(keys[6], 71), 0),
        "row_state": draw_row_state(jax.random.fold_in(keys[6], 71), 0),
        "col_state": draw_col_state(jax.random.fold_in(keys[6], 71), 0),
    }


DECAY = 1.0 - 4.0 ** (-0.8)
TINY = 1e-30
RATE = 0.01

def reference(activations, output_grads, token_counts, weights, row_state, col_state):
    position = jnp.arange(SLOT, dtype=jnp.int32)
    live = (position[None, None, :] < token_counts[:, :, None]).reshape(TOKENS)
    total = jnp.sum(token_counts).astype(jnp.float32)
    grouped = activations.reshape(GROUPS, TOK_DEV, D)
    updates = []
    fresh = []
    row_list = []
    col_list = []
    for matrix in range(2):
        masked = jnp.where(live[:, None], output_grads[matrix], jnp.zeros((), jnp.bfloat16))
        masked = masked.reshape(GROUPS, TOK_DEV, FF)

        def add_group(acc, pair):
            part = jnp.dot(pair[0].T, pair[1], preferred_element_type=jnp.float32)
            return (acc + part, None)
        summed, _ = lax.scan(add_group, jnp.zeros((D, FF), jnp.float32), (grouped, masked))
        grad = summed / total
        square = grad * grad + TINY
        rows_new = DECAY * row_state[matrix] + (1.0 - DECAY) * lax.optimization_barrier(jnp.mean(square, axis=1))
        cols_new = DECAY * col_state[matrix] + (1.0 - DECAY) * lax.optimization_barrier(jnp.mean(square, axis=0))
        scaled = grad / jnp.sqrt(rows_new[:, None] * cols_new[None, :] / jnp.mean(rows_new))
        u_rms = jnp.sqrt(jnp.mean(scaled * scaled))
        w_rms = jnp.sqrt(jnp.mean(weights[matrix] * weights[matrix]))
        step = w_rms * scaled / jnp.maximum(1.0, u_rms)
        updates.append(step)
        fresh.append(weights[matrix] - RATE * step)
        row_list.append(rows_new)
        col_list.append(cols_new)
    return (jnp.stack(updates), jnp.stack(fresh), jnp.stack(row_list), jnp.stack(col_list))
```

```python
import jax
import jax.numpy as jnp
from jax import lax
from jax.experimental import pallas as pl
from jax.experimental.pallas import tpu as pltpu
from jax.sharding import PartitionSpec as P

DECAY = 1.0 - 4.0 ** (-0.8)
TINY = 1e-30
RATE = 0.01
SIDE = 4
ROWS = 64
BLOCK = 2 * ROWS
SCALE = 2.0 ** -15


def gray(i):
    return i ^ (i >> 1)


def turn_kernel(pos_ref, counts_ref, a_ref, out_ref):
    y, x, core = pos_ref[0], pos_ref[1], pos_ref[2]
    tokens = a_ref.shape[0]
    slots = counts_ref.shape[1]
    width = tokens // slots
    lane = lax.broadcasted_iota(jnp.int32, (1, tokens), 1)
    bound = jnp.zeros((1, tokens), jnp.int32)
    for b in range(slots):
        bound = jnp.where(lane // width == b, counts_ref[0, b] + b * width, bound)
    mask = jnp.where(lane < bound, 1.0, 0.0).astype(a_ref.dtype)
    for by in range(SIDE):
        for bx in range(SIDE):
            ry = gray(y) ^ gray(by)
            rx = gray(x) ^ gray(bx)
            x_first = rx * SIDE + ry
            y_first = ry * SIDE + rx
            k = by * SIDE + bx
            t = a_ref[:, k * BLOCK:(k + 1) * BLOCK].T * mask

            @pl.when(core == 0)
            def _():
                out_ref[1, x_first] = t[:ROWS]
                out_ref[0, y_first] = t[ROWS:]

            @pl.when(core == 1)
            def _():
                out_ref[1, y_first] = t[ROWS:]
                out_ref[0, x_first] = t[:ROWS]


def turn(pos, counts, activations):
    tokens, depth = activations.shape
    return pl.pallas_call(
        turn_kernel,
        out_shape=jax.ShapeDtypeStruct((2, SIDE * SIDE, ROWS, tokens), activations.dtype),
        in_specs=[
            pl.BlockSpec(memory_space=pltpu.SMEM),
            pl.BlockSpec(memory_space=pltpu.SMEM),
            pl.BlockSpec(memory_space=pltpu.VMEM),
        ],
        out_specs=pl.BlockSpec(memory_space=pltpu.VMEM),
        compiler_params=pltpu.CompilerParams(vmem_limit_bytes=32 * 1024 * 1024),
    )(pos, counts, activations)


def pairing(first, low):
    pairs = []
    for y in range(SIDE):
        for x in range(SIDE):
            for core in range(2):
                along_x = (core == 0) == first
                i = x if along_x else y
                j = i ^ 1 if low else SIDE - 1 - i
                ny, nx = (y, j) if along_x else (j, x)
                pairs.append(((y * SIDE + x) * 2 + core, (ny * SIDE + nx) * 2 + core))
    return pairs


CORES = [(i, i ^ 1) for i in range(2 * SIDE * SIDE)]
STEPS = (
    ((1, (True, True)), (0, (True, False)), (3, (False, True)), (2, (False, False))),
    ((0, (True, False)), (1, (True, True)), (2, (False, False)), (3, (False, True))),
)


def take(t, dim, i):
    return lax.slice_in_dim(t, i, i + 1, axis=dim)


def add(terms):
    total = terms[0]
    for t in terms[1:]:
        total = total + t
    return total


def everyone(v, axis):
    n = lax.axis_size(axis)
    sent = jnp.broadcast_to(v[None], (n,) + v.shape)
    return jnp.sum(lax.all_to_all(sent, axis, 0, 0, tiled=True), axis=0)


def body(activations, output_grads, token_counts, weights, row_state, col_state):
    ff_dev = output_grads.shape[2]
    rows_all = activations.shape[1]
    cols_all = ff_dev * lax.axis_size("mp")
    dp = lax.axis_index("dp")
    pos = jnp.stack([dp // (2 * SIDE), dp // 2 % SIDE, dp % 2]).astype(jnp.int32)
    turned = turn(pos, token_counts, activations).reshape(2, SIDE * SIDE * ROWS, -1)
    half = ff_dev // 2
    shape = (2, 2, 2, 2, ROWS, half)
    pieces = []
    for matrix in range(2):
        for piece in range(2):
            g = output_grads[matrix, :, piece * half:(piece + 1) * half]
            theirs = jnp.dot(turned[0], g, preferred_element_type=jnp.float32)
            mine = jnp.dot(turned[1], g, preferred_element_type=jnp.float32)
            got = lax.ppermute(theirs, "dp", CORES)
            terms = [mine.reshape(shape), got.reshape(shape)]
            for dim, kind in STEPS[piece]:
                send = add([take(t, dim, 1) for t in terms])
                terms = [take(t, dim, 0) for t in terms]
                terms.append(lax.ppermute(send, "dp", pairing(*kind)))
            pieces.append(add(terms).reshape(ROWS, half))
    summed = jnp.stack(
        [jnp.concatenate(pieces[:2], axis=1), jnp.concatenate(pieces[2:], axis=1)]
    )

    scaled = summed * SCALE
    square = scaled * scaled
    count = jnp.sum(token_counts).astype(jnp.float32)
    cols_part = jnp.concatenate(
        [jnp.sum(square, axis=1).reshape(-1), jnp.full((128,), count)]
    )
    cols_got = everyone(cols_part, "dp")
    total = cols_got[2 * ff_dev]
    back = 1.0 / (total * SCALE)
    cols_sum = cols_got[:2 * ff_dev].reshape(2, ff_dev) * (back * back)
    cols_new = DECAY * col_state + (1.0 - DECAY) * (cols_sum / rows_all + TINY)

    grad = scaled * back
    over_cols = jnp.sum(grad * grad / cols_new[:, None, :], axis=2)
    rows_part = jnp.sum(grad * grad, axis=2)
    weight_sq = jnp.sum(weights * weights, axis=(1, 2))
    small = jnp.concatenate([over_cols.reshape(-1), rows_part.reshape(-1), jnp.repeat(weight_sq, 64)])
    small_got = everyone(small, "mp")
    rows_sum = small_got[2 * ROWS:4 * ROWS].reshape(2, ROWS)
    rows_new = DECAY * row_state + (1.0 - DECAY) * (rows_sum / cols_all + TINY)
    ratio = small_got[:2 * ROWS].reshape(2, ROWS) / rows_new
    weight_z = small_got[4 * ROWS:].reshape(2, 64)[:, 0]
    last = jnp.concatenate([jnp.sum(ratio, axis=1), jnp.sum(rows_new, axis=1), weight_z])
    last_got = everyone(jnp.pad(last, (0, 122)), "dp")
    ratio_tot, rows_tot, weight_tot = last_got[0:2], last_got[2:4], last_got[4:6]
    mean_rows = rows_tot / rows_all
    elements = float(rows_all) * float(cols_all)
    u_rms = jnp.sqrt(ratio_tot * mean_rows / elements)
    w_rms = jnp.sqrt(weight_tot / elements)
    factor = w_rms / jnp.maximum(1.0, u_rms)
    unit = grad / jnp.sqrt(rows_new[:, :, None] * cols_new[:, None, :] / mean_rows[:, None, None])
    update = unit * factor[:, None, None]
    new_weights = weights - RATE * update
    return (update, new_weights, rows_new, cols_new)


def solution(mesh):
    in_specs = (
        P("dp", None),
        P(None, "dp", "mp"),
        P("dp", None),
        P(None, "dp", "mp"),
        P(None, "dp"),
        P(None, "mp"),
    )
    out_specs = (P(None, "dp", "mp"), P(None, "dp", "mp"), P(None, "dp"), P(None, "mp"))
    return jax.shard_map(body, mesh=mesh, in_specs=in_specs, out_specs=out_specs, check_vma=False)
```

```python
import functools

import jax
import jax.numpy as jnp
from jax import lax
from jax.experimental import pallas as pl
from jax.experimental.pallas import tpu as pltpu
from jax.sharding import PartitionSpec as P

DECAY = 1.0 - 4.0 ** (-0.8)
TINY = 1e-30
RATE = 0.01
SIDE = 4
ROWS = 64
BLOCK = 2 * ROWS
LANES = 128
SLOTS = 4
SCALE = 2.0 ** -15


def gray(i):
    return i ^ (i >> 1)


def turn_kernel(info_ref, a_ref, theirs_ref, mine_ref):
    y, x, core = info_ref[0], info_ref[1], info_ref[2]
    tokens = a_ref.shape[0]
    width = tokens // SLOTS
    lane = lax.broadcasted_iota(jnp.int32, (1, tokens), 1)
    bound = jnp.zeros((1, tokens), jnp.int32)
    for b in range(SLOTS):
        bound = jnp.where(lane // width == b, info_ref[3 + b] + b * width, bound)
    mask = jnp.where(lane < bound, 1.0, 0.0).astype(a_ref.dtype)
    for by in range(SIDE):
        for bx in range(SIDE):
            rx = gray(x) ^ gray(bx)
            ry = gray(y) ^ gray(by)
            x_first = rx * SIDE + ry
            y_first = ry * SIDE + rx
            k = by * SIDE + bx
            t = a_ref[:, k * BLOCK:(k + 1) * BLOCK].T * mask

            @pl.when(core == 0)
            def _():
                mine_ref[x_first] = t[:ROWS]
                theirs_ref[y_first] = t[ROWS:]

            @pl.when(core == 1)
            def _():
                mine_ref[y_first] = t[ROWS:]
                theirs_ref[x_first] = t[:ROWS]


VMEM = pl.BlockSpec(memory_space=pltpu.VMEM)
SMEM = pl.BlockSpec(memory_space=pltpu.SMEM)
LIMIT = 24 * 1024 * 1024


def call(kernel, out_shape, in_specs, flops=0, moved=0):
    several = isinstance(out_shape, tuple)
    return pl.pallas_call(
        kernel,
        out_shape=out_shape,
        in_specs=in_specs,
        out_specs=(VMEM,) * len(out_shape) if several else VMEM,
        cost_estimate=pl.CostEstimate(flops=flops, bytes_accessed=moved, transcendentals=0),
        compiler_params=pltpu.CompilerParams(vmem_limit_bytes=LIMIT),
    )


def turn(info, activations):
    tokens, depth = activations.shape
    turned = jax.ShapeDtypeStruct((SIDE * SIDE, ROWS, tokens), activations.dtype)
    return call(turn_kernel, (turned, turned), [SMEM, VMEM], moved=8 * 1024 * 1024)(
        info, activations
    )


def theirs_kernel(matrix, piece, t_ref, g_ref, out_ref):
    half = out_ref.shape[2]
    g = g_ref[matrix, :, piece * half:(piece + 1) * half]
    for q in range(4):
        out_ref[q] = jnp.dot(t_ref[q], g, preferred_element_type=jnp.float32)


def mine_kernel(matrix, piece, t_ref, g_ref, got_ref, send_ref, keep_ref):
    half = send_ref.shape[2]
    g = g_ref[matrix, :, piece * half:(piece + 1) * half]
    keep, send = PARTS[piece]
    for dst, order in ((send_ref, send), (keep_ref, keep)):
        for k, q in enumerate(order):
            dst[k] = jnp.dot(t_ref[q], g, preferred_element_type=jnp.float32) + got_ref[q]


def onward_kernel(keep_ref, got_ref, out_ref):
    out_ref[...] = keep_ref[1] + got_ref[1]


def across_kernel(piece, *refs):
    send_ref, keep_ref = refs[6:]
    keep, send = PARTS[piece]
    for m in range(2):
        kept, got, last = refs[3 * m:3 * m + 3]
        for dst, order in ((send_ref, send), (keep_ref, keep)):
            for k, q in enumerate(order):
                rows = slice(q * ROWS, (q + 1) * ROWS)
                dst[m, k] = kept[0, rows] + got[0, rows] + last[rows]


def forward_kernel(keep_ref, got_ref, out_ref):
    out_ref[...] = keep_ref[:, 1] + got_ref[:, 1]


def chunks(ref):
    return [slice(k * LANES, (k + 1) * LANES) for k in range(ref.shape[-1] // LANES)]


def columns_kernel(info_ref, *refs):
    scaled_ref, part_ref = refs[6:]
    half = scaled_ref.shape[2] // 2
    lists = scaled_ref.shape[2] // LANES
    count = info_ref[3]
    for b in range(1, SLOTS):
        count += info_ref[3 + b]
    for m in range(2):
        for k, cols in enumerate(chunks(scaled_ref)):
            piece, at = divmod(k * LANES, half)
            kept, got, last = refs[3 * piece:3 * piece + 3]
            there = slice(at, at + LANES)
            s = (kept[m, 0, :, there] + got[m, 0, :, there] + last[m, :, there]) * SCALE
            scaled_ref[m, :, cols] = s
            row = jnp.sum(s * s, axis=0, keepdims=True)
            part_ref[:, m * lists + k, :] = jnp.broadcast_to(row, (part_ref.shape[0], LANES))
    tail = (part_ref.shape[0], part_ref.shape[1] - 2 * lists, LANES)
    part_ref[:, 2 * lists:, :] = jnp.full(tail, count.astype(jnp.float32))


def diagonal(n):
    shape = (n, n)
    return lax.broadcasted_iota(jnp.int32, shape, 0) == lax.broadcasted_iota(jnp.int32, shape, 1)


def to_row(column):
    return jnp.sum(jnp.where(diagonal(column.shape[0]), column, 0.0), axis=0, keepdims=True)


def to_column(row):
    return jnp.sum(jnp.where(diagonal(row.shape[1]), row, 0.0), axis=1, keepdims=True)


def rows_kernel(rows_all, part_ref, scaled_ref, state_ref, weights_ref, grad_ref, cols_ref, out_ref):
    lists = scaled_ref.shape[2] // LANES
    summed = jnp.sum(part_ref[...], axis=0)
    total = summed[2 * lists:2 * lists + 1]
    back = 1.0 / (total * SCALE)
    over, square, weight = [], [], []
    lane = lax.broadcasted_iota(jnp.int32, (1, LANES), 1)
    for m in range(2):
        zero = jnp.zeros((ROWS, LANES), jnp.float32)
        acc_over, acc_square, acc_weight = zero, zero, zero
        for k, cols in enumerate(chunks(scaled_ref)):
            mean = summed[m * lists + k:m * lists + k + 1] * (back * back) * (1.0 / rows_all) + TINY
            new = DECAY * state_ref[m:m + 1, cols] + (1.0 - DECAY) * mean
            cols_ref[m:m + 1, cols] = new
            grad = scaled_ref[m, :, cols] * back
            grad_ref[m, :, cols] = grad
            acc_square += grad * grad
            acc_over += grad * grad * (1.0 / new)
            w = weights_ref[m, :, cols]
            acc_weight += w * w
        over.append(jnp.sum(acc_over, axis=1, keepdims=True))
        square.append(jnp.sum(acc_square, axis=1, keepdims=True))
        both = jnp.sum(jnp.sum(acc_weight, axis=0, keepdims=True), axis=1, keepdims=True)
        weight.append(jnp.where(lane == m * ROWS, both, 0.0))
    lines = [to_row(jnp.concatenate(over, axis=0)), to_row(jnp.concatenate(square, axis=0))]
    lines.append(weight[0] + weight[1])
    for k in range(out_ref.shape[1]):
        line = lines[k] if k < len(lines) else jnp.zeros((1, LANES), jnp.float32)
        out_ref[:, k, :] = jnp.broadcast_to(line, (out_ref.shape[0], LANES))


def totals_kernel(cols_all, part_ref, state_ref, rows_ref, out_ref):
    summed = jnp.sum(part_ref[...], axis=0)
    new = DECAY * state_ref[...] + (1.0 - DECAY) * (summed[1:2] * (1.0 / cols_all) + TINY)
    rows_ref[...] = new
    lane = lax.broadcasted_iota(jnp.int32, (1, LANES), 1)
    line = jnp.zeros((1, LANES), jnp.float32)
    for k, values in enumerate((summed[0:1] / new, new, summed[2:3])):
        for m in range(2):
            mine = (lane >= m * ROWS) & (lane < (m + 1) * ROWS)
            one = jnp.sum(jnp.where(mine, values, 0.0), axis=1, keepdims=True)
            line = jnp.where(lane == 2 * k + m, one, line)
    out_ref[...] = jnp.broadcast_to(line, out_ref.shape)


def update_kernel(rows_all, elements, part_ref, rows_ref, cols_ref, grad_ref, weights_ref, update_ref, new_ref):
    summed = jnp.sum(part_ref[...], axis=0, keepdims=True)
    rows = to_column(rows_ref[...])
    for m in range(2):
        ratio, rows_tot, weight = (summed[:, 2 * k + m:2 * k + m + 1] for k in range(3))
        mean_rows = rows_tot * (1.0 / rows_all)
        u_rms = jnp.sqrt(ratio * mean_rows * (1.0 / elements))
        w_rms = jnp.sqrt(weight * (1.0 / elements))
        factor = w_rms / jnp.maximum(1.0, u_rms)
        inverse = 1.0 / mean_rows
        here = rows[m * ROWS:(m + 1) * ROWS]
        for cols in chunks(grad_ref):
            second = here * cols_ref[m:m + 1, cols] * inverse
            step = grad_ref[m, :, cols] * lax.rsqrt(second) * factor
            update_ref[m, :, cols] = step
            new_ref[m, :, cols] = weights_ref[m, :, cols] - RATE * step


def pairing(first, low):
    pairs = []
    for y in range(SIDE):
        for x in range(SIDE):
            for core in range(2):
                along_x = (core == 0) == first
                i = x if along_x else y
                j = i ^ 1 if low else SIDE - 1 - i
                ny, nx = (y, j) if along_x else (j, x)
                pairs.append(((y * SIDE + x) * 2 + core, (ny * SIDE + nx) * 2 + core))
    return pairs


CORES = [(i, i ^ 1) for i in range(2 * SIDE * SIDE)]
PARTS = (((0, 2), (1, 3)), ((0, 1), (2, 3)))


def after(x, *earlier):
    return lax.optimization_barrier((x, *earlier))[0]


def body(activations, output_grads, token_counts, weights, row_state, col_state):
    ff_dev = output_grads.shape[2]
    rows_all = activations.shape[1]
    cols_all = ff_dev * lax.axis_size("mp")
    dp = lax.axis_index("dp")
    pos = jnp.stack([dp // (2 * SIDE), dp // 2 % SIDE, dp % 2]).astype(jnp.int32)
    info = jnp.concatenate([pos, token_counts[0]])
    theirs, mine = turn(info, activations)
    half = ff_dev // 2
    quarter = SIDE * ROWS
    theirs = theirs.reshape(4, quarter, -1)
    mine = mine.reshape(4, quarter, -1)
    whole = jax.ShapeDtypeStruct((4, quarter, half), jnp.float32)
    two = jax.ShapeDtypeStruct((2, quarter, half), jnp.float32)
    one = jax.ShapeDtypeStruct((quarter, half), jnp.float32)
    pieces = 4
    got = [None] * pieces
    sent = [None] * pieces
    kept = [None] * pieces
    out = [None] * pieces

    def swap(i, *earlier):
        kernel = functools.partial(theirs_kernel, *divmod(i, 2))
        out[i] = call(kernel, whole, [VMEM] * 2)(after(theirs, *earlier), output_grads)
        got[i] = lax.ppermute(out[i], "dp", CORES)

    def first(i, *earlier):
        kernel = functools.partial(mine_kernel, *divmod(i, 2))
        sent[i], kept[i] = call(kernel, (two, two), [VMEM] * 3)(
            after(mine, *earlier), output_grads, got[i]
        )
        got[i] = lax.ppermute(sent[i], "dp", pairing(True, i % 2 == 0))

    swap(0)
    for i in range(1, pieces):
        swap(i, out[i - 1])
    first(0, out[3])
    for i in range(1, pieces):
        first(i, sent[i - 1])
    last = sent[3]
    final = [None] * pieces
    for i in range(pieces):
        last = call(onward_kernel, one, [VMEM] * 2)(kept[i], after(got[i], last))
        final[i] = lax.ppermute(last, "dp", pairing(True, i % 2 == 1))
    sides = jax.ShapeDtypeStruct((2, 2, ROWS, half), jnp.float32)
    side = jax.ShapeDtypeStruct((2, ROWS, half), jnp.float32)
    held = []
    for p in range(2):
        terms = [t for i in (p, p + 2) for t in (kept[i], got[i], final[i])]
        terms[0] = after(terms[0], last)
        last, keep = call(functools.partial(across_kernel, p), (sides, sides), [VMEM] * 6)(*terms)
        held.append([keep, lax.ppermute(last, "dp", pairing(False, p == 0))])
    for p in range(2):
        keep, came = held[p]
        last = call(forward_kernel, side, [VMEM] * 2)(keep, after(came, last))
        held[p].append(lax.ppermute(last, "dp", pairing(False, p == 1)))

    f32 = jnp.float32
    mine_shape = jax.ShapeDtypeStruct((2, ROWS, ff_dev), f32)
    lists = 2 * ff_dev // LANES + 8
    dp_n, mp_n = lax.axis_size("dp"), lax.axis_size("mp")
    scaled, part = call(
        columns_kernel,
        (mine_shape, jax.ShapeDtypeStruct((dp_n, lists, LANES), f32)),
        [SMEM] + [VMEM] * 6,
    )(info, *held[0], *held[1])
    part = lax.all_to_all(part, "dp", 0, 0, tiled=True)
    grad, cols_new, part = call(
        functools.partial(rows_kernel, rows_all),
        (mine_shape, jax.ShapeDtypeStruct((2, ff_dev), f32), jax.ShapeDtypeStruct((mp_n, 8, LANES), f32)),
        [VMEM] * 4,
    )(part, scaled, col_state, weights)
    part = lax.all_to_all(part, "mp", 0, 0, tiled=True)
    rows_new, part = call(
        functools.partial(totals_kernel, cols_all),
        (jax.ShapeDtypeStruct((1, LANES), f32), jax.ShapeDtypeStruct((dp_n, LANES), f32)),
        [VMEM] * 2,
    )(part, row_state.reshape(1, LANES))
    part = lax.all_to_all(part, "dp", 0, 0, tiled=True)
    update, new_weights = call(
        functools.partial(update_kernel, rows_all, rows_all * cols_all),
        (mine_shape, mine_shape),
        [VMEM] * 5,
    )(part, rows_new, cols_new, grad, weights)
    return (update, new_weights, rows_new.reshape(2, ROWS), cols_new)


def solution(mesh):
    in_specs = (
        P("dp", None),
        P(None, "dp", "mp"),
        P("dp", None),
        P(None, "dp", "mp"),
        P(None, "dp"),
        P(None, "mp"),
    )
    out_specs = (P(None, "dp", "mp"), P(None, "dp", "mp"), P(None, "dp"), P(None, "mp"))
    return jax.shard_map(body, mesh=mesh, in_specs=in_specs, out_specs=out_specs, check_vma=False)
```

```python
import functools

import jax
import jax.numpy as jnp
from jax import lax
from jax.experimental import pallas as pl
from jax.experimental.pallas import tpu as pltpu
from jax.sharding import PartitionSpec as P

DECAY = 1.0 - 4.0 ** (-0.8)
TINY = 1e-30
RATE = 0.01
SIDE = 4
ROWS = 64
BLOCK = 2 * ROWS
LANES = 128
SLOTS = 4
SCALE = 2.0 ** -15


def gray(i):
    return i ^ (i >> 1)


def turn_kernel(pos_ref, counts_hbm, a_hbm, theirs_ref, mine_ref, counts_ref, a_ref, counts_sem, a_sems):
    tokens, depth = a_ref.shape

    def fetch(i):
        at = (slice(None), pl.ds(i * BLOCK, BLOCK))
        return pltpu.make_async_copy(a_hbm.at[at], a_ref.at[at], a_sems.at[i])

    counts_copy = pltpu.make_async_copy(counts_hbm, counts_ref, counts_sem)
    counts_copy.start()
    for i in range(SIDE * SIDE):
        fetch(i).start()
    y, x, core = pos_ref[0], pos_ref[1], pos_ref[2]
    width = tokens // SLOTS
    lane = lax.broadcasted_iota(jnp.int32, (1, tokens), 1)
    bound = jnp.zeros((1, tokens), jnp.int32)
    counts_copy.wait()
    for b in range(SLOTS):
        bound = jnp.where(lane // width == b, counts_ref[0, b] + b * width, bound)
    mask = jnp.where(lane < bound, 1.0, 0.0).astype(a_ref.dtype)
    for by in range(SIDE):
        for bx in range(SIDE):
            rx = gray(x) ^ gray(bx)
            ry = gray(y) ^ gray(by)
            x_first = rx * SIDE + ry
            y_first = ry * SIDE + rx
            k = by * SIDE + bx
            fetch(k).wait()
            t = a_ref[:, k * BLOCK:(k + 1) * BLOCK].T * mask

            @pl.when(core == 0)
            def _():
                mine_ref[x_first] = t[:ROWS]
                theirs_ref[y_first] = t[ROWS:]

            @pl.when(core == 1)
            def _():
                mine_ref[y_first] = t[ROWS:]
                theirs_ref[x_first] = t[:ROWS]


VMEM = pl.BlockSpec(memory_space=pltpu.VMEM)
SMEM = pl.BlockSpec(memory_space=pltpu.SMEM)
LIMIT = 24 * 1024 * 1024
TURN_LIMIT = 49 * 1024 * 1024


def call(kernel, out_shape, in_specs, flops=0, moved=0):
    several = isinstance(out_shape, tuple)
    return pl.pallas_call(
        kernel,
        out_shape=out_shape,
        in_specs=in_specs,
        out_specs=(VMEM,) * len(out_shape) if several else VMEM,
        cost_estimate=pl.CostEstimate(flops=flops, bytes_accessed=moved, transcendentals=0),
        compiler_params=pltpu.CompilerParams(vmem_limit_bytes=LIMIT),
    )


def turn(pos, counts, activations):
    tokens, depth = activations.shape
    turned = jax.ShapeDtypeStruct((SIDE * SIDE, ROWS, tokens), activations.dtype)
    far = pl.BlockSpec(memory_space=pltpu.HBM)
    return pl.pallas_call(
        turn_kernel,
        out_shape=(turned, turned),
        in_specs=[SMEM, far, far],
        out_specs=(VMEM, VMEM),
        scratch_shapes=[
            pltpu.SMEM(counts.shape, counts.dtype),
            pltpu.VMEM((tokens, depth), activations.dtype),
            pltpu.SemaphoreType.DMA,
            pltpu.SemaphoreType.DMA((SIDE * SIDE,)),
        ],
        cost_estimate=pl.CostEstimate(flops=0, bytes_accessed=8 * 1024 * 1024, transcendentals=0),
        compiler_params=pltpu.CompilerParams(vmem_limit_bytes=TURN_LIMIT),
    )(pos, counts, activations)


def theirs_kernel(matrix, piece, t_ref, g_ref, out_ref):
    half = out_ref.shape[2]
    g = g_ref[matrix, :, piece * half:(piece + 1) * half]
    for q in range(4):
        out_ref[q] = jnp.dot(t_ref[q], g, preferred_element_type=jnp.float32)


def mine_kernel(matrix, piece, t_ref, g_ref, got_ref, send_ref, keep_ref):
    half = send_ref.shape[2]
    g = g_ref[matrix, :, piece * half:(piece + 1) * half]
    keep, send = PARTS[piece]
    for dst, order in ((send_ref, send), (keep_ref, keep)):
        for k, q in enumerate(order):
            dst[k] = jnp.dot(t_ref[q], g, preferred_element_type=jnp.float32) + got_ref[q]


def onward_kernel(keep_ref, got_ref, out_ref):
    out_ref[...] = keep_ref[1] + got_ref[1]


def across_kernel(piece, kept_ref, got_ref, last_ref, send_ref, keep_ref):
    keep, send = PARTS[piece]
    for dst, order in ((send_ref, send), (keep_ref, keep)):
        for k, q in enumerate(order):
            rows = slice(q * ROWS, (q + 1) * ROWS)
            dst[k] = kept_ref[0, rows] + got_ref[0, rows] + last_ref[rows]


def chunks(ref):
    return [slice(k * LANES, (k + 1) * LANES) for k in range(ref.shape[-1] // LANES)]


def columns_kernel(counts_ref, *refs):
    scaled_ref, part_ref = refs[12:]
    half = scaled_ref.shape[2] // 2
    lists = scaled_ref.shape[2] // LANES
    count = counts_ref[0, 0]
    for b in range(1, SLOTS):
        count += counts_ref[0, b]
    for m in range(2):
        for k, cols in enumerate(chunks(scaled_ref)):
            piece, at = divmod(k * LANES, half)
            kept, got, last = refs[6 * m + 3 * piece:6 * m + 3 * piece + 3]
            there = slice(at, at + LANES)
            s = (kept[0, :, there] + got[0, :, there] + last[:, there]) * SCALE
            scaled_ref[m, :, cols] = s
            row = jnp.sum(s * s, axis=0, keepdims=True)
            part_ref[:, m * lists + k, :] = jnp.broadcast_to(row, (part_ref.shape[0], LANES))
    tail = (part_ref.shape[0], part_ref.shape[1] - 2 * lists, LANES)
    part_ref[:, 2 * lists:, :] = jnp.full(tail, count.astype(jnp.float32))


def diagonal(n):
    shape = (n, n)
    return lax.broadcasted_iota(jnp.int32, shape, 0) == lax.broadcasted_iota(jnp.int32, shape, 1)


def to_row(column):
    return jnp.sum(jnp.where(diagonal(column.shape[0]), column, 0.0), axis=0, keepdims=True)


def to_column(row):
    return jnp.sum(jnp.where(diagonal(row.shape[1]), row, 0.0), axis=1, keepdims=True)


def rows_kernel(rows_all, part_ref, scaled_ref, state_ref, weights_ref, grad_ref, cols_ref, out_ref):
    lists = scaled_ref.shape[2] // LANES
    summed = jnp.sum(part_ref[...], axis=0)
    total = summed[2 * lists:2 * lists + 1]
    back = 1.0 / (total * SCALE)
    over, square, weight = [], [], []
    lane = lax.broadcasted_iota(jnp.int32, (1, LANES), 1)
    for m in range(2):
        zero = jnp.zeros((ROWS, LANES), jnp.float32)
        acc_over, acc_square, acc_weight = zero, zero, zero
        for k, cols in enumerate(chunks(scaled_ref)):
            mean = summed[m * lists + k:m * lists + k + 1] * (back * back) * (1.0 / rows_all) + TINY
            new = DECAY * state_ref[m:m + 1, cols] + (1.0 - DECAY) * mean
            cols_ref[m:m + 1, cols] = new
            grad = scaled_ref[m, :, cols] * back
            grad_ref[m, :, cols] = grad
            acc_square += grad * grad
            acc_over += grad * grad * (1.0 / new)
            w = weights_ref[m, :, cols]
            acc_weight += w * w
        over.append(jnp.sum(acc_over, axis=1, keepdims=True))
        square.append(jnp.sum(acc_square, axis=1, keepdims=True))
        both = jnp.sum(jnp.sum(acc_weight, axis=0, keepdims=True), axis=1, keepdims=True)
        weight.append(jnp.where(lane == m * ROWS, both, 0.0))
    lines = [to_row(jnp.concatenate(over, axis=0)), to_row(jnp.concatenate(square, axis=0))]
    lines.append(weight[0] + weight[1])
    for k in range(out_ref.shape[1]):
        line = lines[k] if k < len(lines) else jnp.zeros((1, LANES), jnp.float32)
        out_ref[:, k, :] = jnp.broadcast_to(line, (out_ref.shape[0], LANES))


def totals_kernel(cols_all, part_ref, state_ref, rows_ref, out_ref):
    summed = jnp.sum(part_ref[...], axis=0)
    new = DECAY * state_ref[...] + (1.0 - DECAY) * (summed[1:2] * (1.0 / cols_all) + TINY)
    rows_ref[...] = new
    lane = lax.broadcasted_iota(jnp.int32, (1, LANES), 1)
    line = jnp.zeros((1, LANES), jnp.float32)
    for k, values in enumerate((summed[0:1] / new, new, summed[2:3])):
        for m in range(2):
            mine = (lane >= m * ROWS) & (lane < (m + 1) * ROWS)
            one = jnp.sum(jnp.where(mine, values, 0.0), axis=1, keepdims=True)
            line = jnp.where(lane == 2 * k + m, one, line)
    out_ref[...] = jnp.broadcast_to(line, out_ref.shape)


def update_kernel(rows_all, elements, part_ref, rows_ref, cols_ref, grad_ref, weights_ref, *out_refs):
    update_ref, new_ref, rows_out_ref, cols_out_ref = out_refs
    cols_out_ref[...] = cols_ref[...]
    for m in range(2):
        rows_out_ref[m:m + 1, :] = rows_ref[:, m * ROWS:(m + 1) * ROWS]
    summed = jnp.sum(part_ref[...], axis=0, keepdims=True)
    rows = to_column(rows_ref[...])
    for m in range(2):
        ratio, rows_tot, weight = (summed[:, 2 * k + m:2 * k + m + 1] for k in range(3))
        mean_rows = rows_tot * (1.0 / rows_all)
        u_rms = jnp.sqrt(ratio * mean_rows * (1.0 / elements))
        w_rms = jnp.sqrt(weight * (1.0 / elements))
        factor = w_rms / jnp.maximum(1.0, u_rms)
        inverse = 1.0 / mean_rows
        here = rows[m * ROWS:(m + 1) * ROWS]
        for cols in chunks(grad_ref):
            second = here * cols_ref[m:m + 1, cols] * inverse
            step = grad_ref[m, :, cols] * lax.rsqrt(second) * factor
            update_ref[m, :, cols] = step
            new_ref[m, :, cols] = weights_ref[m, :, cols] - RATE * step


def pairing(first, low):
    pairs = []
    for y in range(SIDE):
        for x in range(SIDE):
            for core in range(2):
                along_x = (core == 0) == first
                i = x if along_x else y
                j = i ^ 1 if low else SIDE - 1 - i
                ny, nx = (y, j) if along_x else (j, x)
                pairs.append(((y * SIDE + x) * 2 + core, (ny * SIDE + nx) * 2 + core))
    return pairs


CORES = [(i, i ^ 1) for i in range(2 * SIDE * SIDE)]
PARTS = (((0, 2), (1, 3)), ((0, 1), (2, 3)))


def after(x, *earlier):
    return lax.optimization_barrier((x, *earlier))[0]


def body(activations, output_grads, token_counts, weights, row_state, col_state):
    ff_dev = output_grads.shape[2]
    rows_all = activations.shape[1]
    cols_all = ff_dev * lax.axis_size("mp")
    dp = lax.axis_index("dp")
    pos = jnp.stack([dp // (2 * SIDE), dp // 2 % SIDE, dp % 2]).astype(jnp.int32)
    theirs, mine = turn(pos, token_counts, activations)
    half = ff_dev // 2
    quarter = SIDE * ROWS
    theirs = theirs.reshape(4, quarter, -1)
    mine = mine.reshape(4, quarter, -1)
    whole = jax.ShapeDtypeStruct((4, quarter, half), jnp.float32)
    two = jax.ShapeDtypeStruct((2, quarter, half), jnp.float32)
    one = jax.ShapeDtypeStruct((quarter, half), jnp.float32)
    pieces = 4
    got = [None] * pieces
    sent = [None] * pieces
    kept = [None] * pieces
    out = [None] * pieces

    def swap(i, *earlier):
        kernel = functools.partial(theirs_kernel, *divmod(i, 2))
        out[i] = call(kernel, whole, [VMEM] * 2)(after(theirs, *earlier), output_grads)
        got[i] = lax.ppermute(out[i], "dp", CORES)

    def first(i, *earlier):
        kernel = functools.partial(mine_kernel, *divmod(i, 2))
        sent[i], kept[i] = call(kernel, (two, two), [VMEM] * 3)(
            after(mine, *earlier), output_grads, got[i]
        )
        got[i] = lax.ppermute(sent[i], "dp", pairing(True, i % 2 == 0))

    swap(0)
    for i in range(1, pieces):
        swap(i, out[i - 1])
    first(0, out[3])
    for i in range(1, pieces):
        first(i, sent[i - 1])
    last = sent[3]
    final = [None] * pieces
    for i in range(pieces):
        last = call(onward_kernel, one, [VMEM] * 2)(kept[i], after(got[i], last))
        final[i] = lax.ppermute(last, "dp", pairing(True, i % 2 == 1))
    sides = jax.ShapeDtypeStruct((2, ROWS, half), jnp.float32)
    side = jax.ShapeDtypeStruct((ROWS, half), jnp.float32)
    held = []
    for i in range(pieces):
        last, keep = call(functools.partial(across_kernel, i % 2), (sides, sides), [VMEM] * 3)(
            kept[i], got[i], after(final[i], last)
        )
        held.append([keep, lax.ppermute(last, "dp", pairing(False, i % 2 == 0))])
    for i in range(pieces):
        keep, came = held[i]
        last = call(onward_kernel, side, [VMEM] * 2)(keep, after(came, last))
        held[i].append(lax.ppermute(last, "dp", pairing(False, i % 2 == 1)))

    f32 = jnp.float32
    mine_shape = jax.ShapeDtypeStruct((2, ROWS, ff_dev), f32)
    lists = 2 * ff_dev // LANES + 8
    dp_n, mp_n = lax.axis_size("dp"), lax.axis_size("mp")
    scaled, part = call(
        columns_kernel,
        (mine_shape, jax.ShapeDtypeStruct((dp_n, lists, LANES), f32)),
        [SMEM] + [VMEM] * 12,
    )(token_counts, *(t for group in held for t in group))
    part = lax.all_to_all(part, "dp", 0, 0, tiled=True)
    grad, cols_new, part = call(
        functools.partial(rows_kernel, rows_all),
        (mine_shape, jax.ShapeDtypeStruct((2, ff_dev), f32), jax.ShapeDtypeStruct((mp_n, 8, LANES), f32)),
        [VMEM] * 4,
    )(part, scaled, col_state, weights)
    part = lax.all_to_all(part, "mp", 0, 0, tiled=True)
    rows_new, part = call(
        functools.partial(totals_kernel, cols_all),
        (jax.ShapeDtypeStruct((1, LANES), f32), jax.ShapeDtypeStruct((dp_n, LANES), f32)),
        [VMEM] * 2,
    )(part, row_state.reshape(1, LANES))
    part = lax.all_to_all(part, "dp", 0, 0, tiled=True)
    rows_shape, cols_shape = (jax.ShapeDtypeStruct(t.shape, f32) for t in (row_state, col_state))
    return call(
        functools.partial(update_kernel, rows_all, rows_all * cols_all),
        (mine_shape, mine_shape, rows_shape, cols_shape),
        [VMEM] * 5,
    )(part, rows_new, cols_new, grad, weights)


def solution(mesh):
    in_specs = (
        P("dp", None),
        P(None, "dp", "mp"),
        P("dp", None),
        P(None, "dp", "mp"),
        P(None, "dp"),
        P(None, "mp"),
    )
    out_specs = (P(None, "dp", "mp"), P(None, "dp", "mp"), P(None, "dp"), P(None, "mp"))
    return jax.shard_map(body, mesh=mesh, in_specs=in_specs, out_specs=out_specs, check_vma=False)
```

```python
import functools

import jax
import jax.numpy as jnp
from jax import lax
from jax.experimental import pallas as pl
from jax.experimental.pallas import tpu as pltpu
from jax.sharding import PartitionSpec as P

DECAY = 1.0 - 4.0 ** (-0.8)
TINY = 1e-30
RATE = 0.01
SIDE = 4
ROWS = 64
BLOCK = 2 * ROWS
LANES = 128
SLOTS = 4
SCALE = 2.0 ** -15


def gray(i):
    return i ^ (i >> 1)


def turn_kernel(pos_ref, a_hbm, out_ref, a_ref, sems):
    slot = a_ref.shape[0] // SLOTS

    def fetch(c):
        at = pl.ds(c * slot, slot)
        return pltpu.make_async_copy(a_hbm.at[at], a_ref.at[at], sems.at[c])

    for c in range(SLOTS):
        fetch(c).start()
    y, x, core = pos_ref[0], pos_ref[1], pos_ref[2]
    places = []
    for by in range(SIDE):
        for bx in range(SIDE):
            rx = gray(x) ^ gray(bx)
            ry = gray(y) ^ gray(by)
            places.append((rx * SIDE + ry, ry * SIDE + rx))
    for c in range(SLOTS):
        fetch(c).wait()
        tokens = slice(c * slot, (c + 1) * slot)
        for k, (x_first, y_first) in enumerate(places):
            t = a_ref[tokens, k * BLOCK:(k + 1) * BLOCK].T
            out_ref[1 - core, x_first, :, tokens] = t[:ROWS]
            out_ref[core, y_first, :, tokens] = t[ROWS:]


VMEM = pl.BlockSpec(memory_space=pltpu.VMEM)
SMEM = pl.BlockSpec(memory_space=pltpu.SMEM)
LIMIT = 24 * 1024 * 1024
TURN_LIMIT = 49 * 1024 * 1024


def call(kernel, out_shape, in_specs, flops=0, moved=0):
    several = isinstance(out_shape, tuple)
    return pl.pallas_call(
        kernel,
        out_shape=out_shape,
        in_specs=in_specs,
        out_specs=(VMEM,) * len(out_shape) if several else VMEM,
        cost_estimate=pl.CostEstimate(flops=flops, bytes_accessed=moved, transcendentals=0),
        compiler_params=pltpu.CompilerParams(vmem_limit_bytes=LIMIT),
    )


def turn(pos, activations):
    tokens, depth = activations.shape
    return pl.pallas_call(
        turn_kernel,
        out_shape=jax.ShapeDtypeStruct((2, SIDE * SIDE, ROWS, tokens), activations.dtype),
        in_specs=[SMEM, pl.BlockSpec(memory_space=pltpu.HBM)],
        out_specs=VMEM,
        scratch_shapes=[
            pltpu.VMEM((tokens, depth), activations.dtype),
            pltpu.SemaphoreType.DMA((SLOTS,)),
        ],
        cost_estimate=pl.CostEstimate(flops=0, bytes_accessed=8 * 1024 * 1024, transcendentals=0),
        compiler_params=pltpu.CompilerParams(vmem_limit_bytes=TURN_LIMIT),
    )(pos, activations)


def live(counts_ref, tokens):
    width = tokens // SLOTS
    lane = lax.broadcasted_iota(jnp.int32, (1, tokens), 1)
    bound = jnp.zeros((1, tokens), jnp.int32)
    for b in range(SLOTS):
        bound = jnp.where(lane // width == b, counts_ref[:, b:b + 1] + b * width, bound)
    return jnp.where(lane < bound, 1.0, 0.0).astype(jnp.bfloat16)


def theirs_kernel(matrix, piece, t_ref, counts_ref, g_ref, out_ref):
    half = out_ref.shape[2]
    g = g_ref[matrix, :, piece * half:(piece + 1) * half]
    mask = live(counts_ref, t_ref.shape[-1])
    for q in range(SIDE):
        left = t_ref[0, q] * mask
        out_ref[q] = jnp.dot(left, g, preferred_element_type=jnp.float32)


def mine_kernel(matrix, piece, t_ref, counts_ref, g_ref, got_ref, send_ref, keep_ref):
    half = send_ref.shape[2]
    g = g_ref[matrix, :, piece * half:(piece + 1) * half]
    mask = live(counts_ref, t_ref.shape[-1])
    keep, send = PARTS[piece]
    for dst, order in ((send_ref, send), (keep_ref, keep)):
        for k, q in enumerate(order):
            left = t_ref[1, q] * mask
            dst[k] = jnp.dot(left, g, preferred_element_type=jnp.float32) + got_ref[q]


def onward_kernel(keep_ref, got_ref, out_ref):
    out_ref[...] = keep_ref[1] + got_ref[1]


def across_kernel(piece, kept_ref, got_ref, last_ref, send_ref, keep_ref):
    keep, send = PARTS[piece]
    for dst, order in ((send_ref, send), (keep_ref, keep)):
        for k, q in enumerate(order):
            rows = slice(q * ROWS, (q + 1) * ROWS)
            dst[k] = kept_ref[0, rows] + got_ref[0, rows] + last_ref[rows]


def deal_kernel(*refs):
    outs = refs[6:]
    half = outs[0].shape[1] // 2
    for p in range(2):
        kept_ref, got_ref, last_ref = refs[3 * p:3 * p + 3]
        for q, out_ref in enumerate(outs):
            rows = slice(q * ROWS, (q + 1) * ROWS)
            out_ref[:, p * half:(p + 1) * half] = kept_ref[0, rows] + got_ref[0, rows] + last_ref[rows]


def chunks(ref):
    return [slice(k * LANES, (k + 1) * LANES) for k in range(ref.shape[-1] // LANES)]


def columns_kernel(counts_ref, *refs):
    scaled_ref, part_ref = refs[10:]
    half = scaled_ref.shape[2] // 2
    lists = scaled_ref.shape[2] // LANES

    def summed(m, k):
        if m == 1:
            own, low, high, far = (ref[:, k * LANES:(k + 1) * LANES] for ref in refs[6:10])
            return own + low + high + far
        piece, at = divmod(k * LANES, half)
        kept, got, last = refs[3 * piece:3 * piece + 3]
        there = slice(at, at + LANES)
        return kept[0, :, there] + got[0, :, there] + last[:, there]

    for m in range(2):
        for k, cols in enumerate(chunks(scaled_ref)):
            s = summed(m, k) * SCALE
            scaled_ref[m, :, cols] = s
            row = jnp.sum(s * s, axis=0, keepdims=True)
            part_ref[:, m * lists + k, :] = jnp.broadcast_to(row, (part_ref.shape[0], LANES))
    count = jnp.sum(counts_ref[...].astype(jnp.float32), axis=1, keepdims=True)
    part_ref[:, 2 * lists:, :] = jnp.broadcast_to(count[None], (part_ref.shape[0], 8, LANES))


def diagonal(n):
    shape = (n, n)
    return lax.broadcasted_iota(jnp.int32, shape, 0) == lax.broadcasted_iota(jnp.int32, shape, 1)


def to_row(column):
    return jnp.sum(jnp.where(diagonal(column.shape[0]), column, 0.0), axis=0, keepdims=True)


def to_column(row):
    return jnp.sum(jnp.where(diagonal(row.shape[1]), row, 0.0), axis=1, keepdims=True)


def rows_kernel(rows_all, part_ref, scaled_ref, state_ref, weights_ref, back_ref, cols_ref, out_ref):
    lists = scaled_ref.shape[2] // LANES
    summed = jnp.sum(part_ref[...], axis=0)
    total = summed[2 * lists:2 * lists + 1]
    back = 1.0 / (total * SCALE)
    back_ref[...] = back
    over, square, weight = [], [], []
    lane = lax.broadcasted_iota(jnp.int32, (1, LANES), 1)
    for m in range(2):
        zero = jnp.zeros((ROWS, LANES), jnp.float32)
        acc_over, acc_square, acc_weight = zero, zero, zero
        for k, cols in enumerate(chunks(scaled_ref)):
            mean = summed[m * lists + k:m * lists + k + 1] * (back * back) * (1.0 / rows_all) + TINY
            new = DECAY * state_ref[m:m + 1, cols] + (1.0 - DECAY) * mean
            cols_ref[m:m + 1, cols] = new
            grad = scaled_ref[m, :, cols] * back
            acc_square += grad * grad
            acc_over += grad * grad * (1.0 / new)
            w = weights_ref[m, :, cols]
            acc_weight += w * w
        over.append(jnp.sum(acc_over, axis=1, keepdims=True))
        square.append(jnp.sum(acc_square, axis=1, keepdims=True))
        both = jnp.sum(jnp.sum(acc_weight, axis=0, keepdims=True), axis=1, keepdims=True)
        weight.append(jnp.where(lane == m * ROWS, both, 0.0))
    lines = [to_row(jnp.concatenate(over, axis=0)), to_row(jnp.concatenate(square, axis=0))]
    lines.append(weight[0] + weight[1])
    for k in range(out_ref.shape[1]):
        line = lines[k] if k < len(lines) else jnp.zeros((1, LANES), jnp.float32)
        out_ref[:, k, :] = jnp.broadcast_to(line, (out_ref.shape[0], LANES))


def totals_kernel(cols_all, part_ref, state_ref, rows_ref, out_ref):
    summed = jnp.sum(part_ref[...], axis=0)
    state = to_row(jnp.concatenate([to_column(state_ref[m:m + 1]) for m in range(2)], axis=0))
    new = DECAY * state + (1.0 - DECAY) * (summed[1:2] * (1.0 / cols_all) + TINY)
    rows_ref[...] = new
    lane = lax.broadcasted_iota(jnp.int32, (1, LANES), 1)
    line = jnp.zeros((1, LANES), jnp.float32)
    for k, values in enumerate((summed[0:1] / new, new, summed[2:3])):
        for m in range(2):
            mine = (lane >= m * ROWS) & (lane < (m + 1) * ROWS)
            one = jnp.sum(jnp.where(mine, values, 0.0), axis=1, keepdims=True)
            line = jnp.where(lane == 2 * k + m, one, line)
    out_ref[...] = jnp.broadcast_to(line, out_ref.shape)


def update_kernel(rows_all, elements, *refs):
    part_ref, rows_ref, cols_ref, back_ref, scaled_ref, weights_ref = refs[:6]
    update_ref, new_ref, rows_out_ref, cols_out_ref = refs[6:]
    cols_out_ref[...] = cols_ref[...]
    summed = jnp.sum(part_ref[...], axis=0, keepdims=True)
    rows = to_column(rows_ref[...])
    back = back_ref[...]
    for m in range(2):
        rows_out_ref[m:m + 1, :] = rows_ref[:, m * ROWS:(m + 1) * ROWS]
        ratio, rows_tot, weight = (summed[:, 2 * k + m:2 * k + m + 1] for k in range(3))
        mean_rows = rows_tot * (1.0 / rows_all)
        u_rms = jnp.sqrt(ratio * mean_rows * (1.0 / elements))
        w_rms = jnp.sqrt(weight * (1.0 / elements))
        factor = w_rms / jnp.maximum(1.0, u_rms)
        inverse = 1.0 / mean_rows
        here = rows[m * ROWS:(m + 1) * ROWS]
        for cols in chunks(scaled_ref):
            second = here * cols_ref[m:m + 1, cols] * inverse
            step = scaled_ref[m, :, cols] * back * lax.rsqrt(second) * factor
            update_ref[m, :, cols] = step
            new_ref[m, :, cols] = weights_ref[m, :, cols] - RATE * step


def pairing(first, kind):
    pairs = []
    for y in range(SIDE):
        for x in range(SIDE):
            for core in range(2):
                along_x = (core == 0) == first
                i = x if along_x else y
                j = (i ^ 1, SIDE - 1 - i, (i + 2) % SIDE)[kind]
                ny, nx = (y, j) if along_x else (j, x)
                pairs.append(((y * SIDE + x) * 2 + core, (ny * SIDE + nx) * 2 + core))
    return pairs


CORES = [(i, i ^ 1) for i in range(2 * SIDE * SIDE)]
PARTS = (((0, 2), (1, 3)), ((0, 1), (2, 3)))


def after(x, *earlier):
    return lax.optimization_barrier((x, *earlier))[0]


def body(activations, output_grads, token_counts, weights, row_state, col_state):
    ff_dev = output_grads.shape[2]
    rows_all = activations.shape[1]
    cols_all = ff_dev * lax.axis_size("mp")
    dp = lax.axis_index("dp")
    pos = jnp.stack([dp // (2 * SIDE), dp // 2 % SIDE, dp % 2]).astype(jnp.int32)
    turned = turn(pos, activations)
    tokens = activations.shape[0]
    half = ff_dev // 2
    quarter = SIDE * ROWS
    turned = turned.reshape(2, SIDE, quarter, tokens)
    whole = jax.ShapeDtypeStruct((4, quarter, half), jnp.float32)
    two = jax.ShapeDtypeStruct((2, quarter, half), jnp.float32)
    one = jax.ShapeDtypeStruct((quarter, half), jnp.float32)
    pieces = 4
    got = [None] * pieces
    sent = [None] * pieces
    kept = [None] * pieces
    out = [None] * pieces

    def swap(i, *earlier):
        kernel = functools.partial(theirs_kernel, *divmod(i, 2))
        out[i] = call(kernel, whole, [VMEM] * 3)(after(turned, *earlier), token_counts, output_grads)
        got[i] = lax.ppermute(out[i], "dp", CORES)

    def first(i, *earlier):
        kernel = functools.partial(mine_kernel, *divmod(i, 2))
        sent[i], kept[i] = call(kernel, (two, two), [VMEM] * 4)(
            after(turned, *earlier), token_counts, output_grads, got[i]
        )
        got[i] = lax.ppermute(sent[i], "dp", pairing(True, i % 2))

    swap(0)
    for i in range(1, pieces):
        swap(i, out[i - 1])
    first(0, out[3])
    for i in range(1, pieces):
        first(i, sent[i - 1])
    last = sent[3]
    final = [None] * pieces
    for i in range(pieces):
        last = call(onward_kernel, one, [VMEM] * 2)(kept[i], after(got[i], last))
        final[i] = lax.ppermute(last, "dp", pairing(True, 1 - i % 2))
    sides = jax.ShapeDtypeStruct((2, ROWS, half), jnp.float32)
    side = jax.ShapeDtypeStruct((ROWS, half), jnp.float32)
    share = jax.ShapeDtypeStruct((ROWS, ff_dev), jnp.float32)

    def deal(m):
        nonlocal last
        terms = [t for i in (2 * m, 2 * m + 1) for t in (kept[i], got[i], final[i])]
        terms[0] = after(terms[0], last)
        own, low, high, far = call(deal_kernel, (share,) * 4, [VMEM] * 6)(*terms)
        last = own
        far = lax.ppermute(far, "dp", pairing(False, 2))
        low = lax.ppermute(low, "dp", pairing(False, 0))
        high = lax.ppermute(high, "dp", pairing(False, 1))
        return own, low, high, far

    held = []
    for i in range(2):
        last, keep = call(functools.partial(across_kernel, i % 2), (sides, sides), [VMEM] * 3)(
            kept[i], got[i], after(final[i], last)
        )
        held.append([keep, lax.ppermute(last, "dp", pairing(False, i % 2))])
    dealt = deal(1)
    for i in range(2):
        keep, came = held[i]
        last = call(onward_kernel, side, [VMEM] * 2)(keep, after(came, last))
        held[i].append(lax.ppermute(last, "dp", pairing(False, 1 - i % 2)))

    f32 = jnp.float32
    mine_shape = jax.ShapeDtypeStruct((2, ROWS, ff_dev), f32)
    lists = 2 * ff_dev // LANES + 8
    dp_n, mp_n = lax.axis_size("dp"), lax.axis_size("mp")
    scaled, part = call(
        columns_kernel,
        (mine_shape, jax.ShapeDtypeStruct((dp_n, lists, LANES), f32)),
        [VMEM] * 11,
    )(token_counts, *held[0], *held[1], *dealt)
    part = lax.all_to_all(part, "dp", 0, 0, tiled=True)
    line = jax.ShapeDtypeStruct((1, LANES), f32)
    back, cols_new, part = call(
        functools.partial(rows_kernel, rows_all),
        (line, jax.ShapeDtypeStruct((2, ff_dev), f32), jax.ShapeDtypeStruct((mp_n, 8, LANES), f32)),
        [VMEM] * 4,
    )(part, scaled, col_state, weights)
    part = lax.all_to_all(part, "mp", 0, 0, tiled=True)
    rows_new, part = call(
        functools.partial(totals_kernel, cols_all),
        (line, jax.ShapeDtypeStruct((dp_n, LANES), f32)),
        [VMEM] * 2,
    )(part, row_state)
    part = lax.all_to_all(part, "dp", 0, 0, tiled=True)
    rows_shape, cols_shape = (jax.ShapeDtypeStruct(t.shape, f32) for t in (row_state, col_state))
    return call(
        functools.partial(update_kernel, rows_all, rows_all * cols_all),
        (mine_shape, mine_shape, rows_shape, cols_shape),
        [VMEM] * 6,
    )(part, rows_new, cols_new, back, scaled, weights)


def solution(mesh):
    in_specs = (
        P("dp", None),
        P(None, "dp", "mp"),
        P("dp", None),
        P(None, "dp", "mp"),
        P(None, "dp"),
        P(None, "mp"),
    )
    out_specs = (P(None, "dp", "mp"), P(None, "dp", "mp"), P(None, "dp"), P(None, "mp"))
    return jax.shard_map(body, mesh=mesh, in_specs=in_specs, out_specs=out_specs, check_vma=False)
```

```python
import functools

import jax
import jax.numpy as jnp
from jax import lax
from jax.experimental import pallas as pl
from jax.experimental.pallas import tpu as pltpu
from jax.sharding import PartitionSpec as P

DECAY = 1.0 - 4.0 ** (-0.8)
TINY = 1e-30
RATE = 0.01
SIDE = 4
ROWS = 64
BLOCK = 2 * ROWS
LANES = 128
SLOTS = 4
EXTRA = 8


def gray(i):
    return i ^ (i >> 1)


def turn_kernel(pos_ref, a_hbm, out_ref, a_ref, sems):
    slot = a_ref.shape[0] // SLOTS

    def fetch(c):
        at = pl.ds(c * slot, slot)
        return pltpu.make_async_copy(a_hbm.at[at], a_ref.at[at], sems.at[c])

    for c in range(SLOTS):
        fetch(c).start()
    y, x, core = pos_ref[0], pos_ref[1], pos_ref[2]
    places = []
    for by in range(SIDE):
        for bx in range(SIDE):
            rx = gray(x) ^ gray(bx)
            ry = gray(y) ^ gray(by)
            places.append((rx * SIDE + ry, ry * SIDE + rx))
    for c in range(SLOTS):
        fetch(c).wait()
        tokens = slice(c * slot, (c + 1) * slot)
        for k, (x_first, y_first) in enumerate(places):
            t = a_ref[tokens, k * BLOCK:(k + 1) * BLOCK].T
            out_ref[1 - core, x_first, :, tokens] = t[:ROWS]
            out_ref[core, y_first, :, tokens] = t[ROWS:]


VMEM = pl.BlockSpec(memory_space=pltpu.VMEM)
SMEM = pl.BlockSpec(memory_space=pltpu.SMEM)
LIMIT = 24 * 1024 * 1024
TURN_LIMIT = 49 * 1024 * 1024


def call(kernel, out_shape, in_specs, flops=0, moved=0):
    several = isinstance(out_shape, tuple)
    return pl.pallas_call(
        kernel,
        out_shape=out_shape,
        in_specs=in_specs,
        out_specs=(VMEM,) * len(out_shape) if several else VMEM,
        cost_estimate=pl.CostEstimate(flops=flops, bytes_accessed=moved, transcendentals=0),
        compiler_params=pltpu.CompilerParams(vmem_limit_bytes=LIMIT),
    )


def turn(pos, activations):
    tokens, depth = activations.shape
    return pl.pallas_call(
        turn_kernel,
        out_shape=jax.ShapeDtypeStruct((2, SIDE * SIDE, ROWS, tokens), activations.dtype),
        in_specs=[SMEM, pl.BlockSpec(memory_space=pltpu.HBM)],
        out_specs=VMEM,
        scratch_shapes=[
            pltpu.VMEM((tokens, depth), activations.dtype),
            pltpu.SemaphoreType.DMA((SLOTS,)),
        ],
        cost_estimate=pl.CostEstimate(flops=0, bytes_accessed=8 * 1024 * 1024, transcendentals=0),
        compiler_params=pltpu.CompilerParams(vmem_limit_bytes=TURN_LIMIT),
    )(pos, activations)


def live(counts_ref, tokens):
    width = tokens // SLOTS
    lane = lax.broadcasted_iota(jnp.int32, (1, tokens), 1)
    bound = jnp.zeros((1, tokens), jnp.int32)
    for b in range(SLOTS):
        bound = jnp.where(lane // width == b, counts_ref[:, b:b + 1] + b * width, bound)
    return jnp.where(lane < bound, 1.0, 0.0).astype(jnp.bfloat16)


def counted(counts_ref, out_ref):
    count = jnp.sum(counts_ref[...].astype(jnp.float32), axis=1, keepdims=True)
    return jnp.broadcast_to(count, (EXTRA, out_ref.shape[1]))


def theirs_kernel(matrix, piece, t_ref, counts_ref, g_ref, out_ref):
    half = out_ref.shape[1]
    quarter = t_ref.shape[2]
    g = g_ref[matrix, :, piece * half:(piece + 1) * half]
    mask = live(counts_ref, t_ref.shape[-1])
    for q in range(SIDE):
        left = t_ref[0, q] * mask
        rows = slice(q * quarter, (q + 1) * quarter)
        out_ref[rows] = jnp.dot(left, g, preferred_element_type=jnp.float32)
    if out_ref.shape[0] > SIDE * quarter:
        out_ref[SIDE * quarter:] = counted(counts_ref, out_ref)


def mine_kernel(matrix, piece, t_ref, counts_ref, g_ref, got_ref, send_ref, keep_ref):
    half = send_ref.shape[1]
    quarter = t_ref.shape[2]
    g = g_ref[matrix, :, piece * half:(piece + 1) * half]
    mask = live(counts_ref, t_ref.shape[-1])
    keep, send = PARTS[piece]
    for dst, order in ((send_ref, send), (keep_ref, keep)):
        for k, q in enumerate(order):
            left = t_ref[1, q] * mask
            came = got_ref[q * quarter:(q + 1) * quarter]
            product = jnp.dot(left, g, preferred_element_type=jnp.float32)
            dst[k * quarter:(k + 1) * quarter] = product + came
    if got_ref.shape[0] > SIDE * quarter:
        count = got_ref[SIDE * quarter:] + counted(counts_ref, got_ref)
        send_ref[2 * quarter:] = count
        keep_ref[2 * quarter:] = count


def onward_kernel(rows, keep_ref, got_ref, out_ref):
    out_ref[:rows] = keep_ref[rows:2 * rows] + got_ref[rows:2 * rows]
    if out_ref.shape[0] > rows:
        out_ref[rows:] = keep_ref[2 * rows:] + got_ref[2 * rows:]


def across_kernel(piece, kept_ref, got_ref, last_ref, send_ref, keep_ref):
    keep, send = PARTS[piece]
    for dst, order in ((send_ref, send), (keep_ref, keep)):
        for k, q in enumerate(order):
            rows = slice(q * ROWS, (q + 1) * ROWS)
            dst[k * ROWS:(k + 1) * ROWS] = kept_ref[rows] + got_ref[rows] + last_ref[rows]
    if send_ref.shape[0] > 2 * ROWS:
        count = kept_ref[-EXTRA:] + got_ref[-EXTRA:] + last_ref[-EXTRA:]
        send_ref[2 * ROWS:] = count
        keep_ref[2 * ROWS:] = count


def deal_kernel(*refs):
    outs = refs[6:]
    half = outs[0].shape[1] // 2
    for p in range(2):
        kept_ref, got_ref, last_ref = refs[3 * p:3 * p + 3]
        for q, out_ref in enumerate(outs):
            rows = slice(q * ROWS, (q + 1) * ROWS)
            out_ref[:, p * half:(p + 1) * half] = kept_ref[rows] + got_ref[rows] + last_ref[rows]


def chunks(ref):
    return [slice(k * LANES, (k + 1) * LANES) for k in range(ref.shape[-1] // LANES)]


def columns_kernel(*refs):
    grad_ref, part_ref = refs[10:]
    half = grad_ref.shape[2] // 2
    lists = grad_ref.shape[2] // LANES
    total = sum(ref[-EXTRA:][:1, :LANES] for ref in refs[:3])
    back = 1.0 / total

    def summed(m, k):
        if m == 1:
            own, low, high, far = (ref[:, k * LANES:(k + 1) * LANES] for ref in refs[6:10])
            return own + low + high + far
        piece, at = divmod(k * LANES, half)
        there = slice(at, at + LANES)
        kept, got, last = (ref[:ROWS, there] for ref in refs[3 * piece:3 * piece + 3])
        return kept + got + last

    for m in range(2):
        for k, cols in enumerate(chunks(grad_ref)):
            grad = summed(m, k) * back
            grad_ref[m, :, cols] = grad
            row = jnp.sum(grad * grad, axis=0, keepdims=True)
            part_ref[:, m * lists + k, :] = jnp.broadcast_to(row, (part_ref.shape[0], LANES))


def diagonal(n):
    shape = (n, n)
    return lax.broadcasted_iota(jnp.int32, shape, 0) == lax.broadcasted_iota(jnp.int32, shape, 1)


def to_row(column):
    return jnp.sum(jnp.where(diagonal(column.shape[0]), column, 0.0), axis=0, keepdims=True)


def to_column(row):
    return jnp.sum(jnp.where(diagonal(row.shape[1]), row, 0.0), axis=1, keepdims=True)


def rows_kernel(rows_all, part_ref, grad_ref, state_ref, weights_ref, cols_ref, out_ref):
    lists = grad_ref.shape[2] // LANES
    summed = jnp.sum(part_ref[...], axis=0)
    over, square, weight = [], [], []
    lane = lax.broadcasted_iota(jnp.int32, (1, LANES), 1)
    for m in range(2):
        zero = jnp.zeros((ROWS, LANES), jnp.float32)
        acc_over, acc_square, acc_weight = zero, zero, zero
        for k, cols in enumerate(chunks(grad_ref)):
            mean = summed[m * lists + k:m * lists + k + 1] * (1.0 / rows_all) + TINY
            new = DECAY * state_ref[m:m + 1, cols] + (1.0 - DECAY) * mean
            cols_ref[m:m + 1, cols] = new
            grad = grad_ref[m, :, cols]
            acc_square += grad * grad
            acc_over += grad * grad * (1.0 / new)
            w = weights_ref[m, :, cols]
            acc_weight += w * w
        over.append(jnp.sum(acc_over, axis=1, keepdims=True))
        square.append(jnp.sum(acc_square, axis=1, keepdims=True))
        both = jnp.sum(jnp.sum(acc_weight, axis=0, keepdims=True), axis=1, keepdims=True)
        weight.append(jnp.where(lane == m * ROWS, both, 0.0))
    lines = [to_row(jnp.concatenate(over, axis=0)), to_row(jnp.concatenate(square, axis=0))]
    lines.append(weight[0] + weight[1])
    for k in range(out_ref.shape[1]):
        line = lines[k] if k < len(lines) else jnp.zeros((1, LANES), jnp.float32)
        out_ref[:, k, :] = jnp.broadcast_to(line, (out_ref.shape[0], LANES))


def totals_kernel(cols_all, part_ref, state_ref, rows_ref, out_ref):
    summed = jnp.sum(part_ref[...], axis=0)
    state = to_row(jnp.concatenate([to_column(state_ref[m:m + 1]) for m in range(2)], axis=0))
    new = DECAY * state + (1.0 - DECAY) * (summed[1:2] * (1.0 / cols_all) + TINY)
    rows_ref[...] = new
    lane = lax.broadcasted_iota(jnp.int32, (1, LANES), 1)
    line = jnp.zeros((1, LANES), jnp.float32)
    for k, values in enumerate((summed[0:1] / new, new, summed[2:3])):
        for m in range(2):
            mine = (lane >= m * ROWS) & (lane < (m + 1) * ROWS)
            one = jnp.sum(jnp.where(mine, values, 0.0), axis=1, keepdims=True)
            line = jnp.where(lane == 2 * k + m, one, line)
    out_ref[...] = jnp.broadcast_to(line, out_ref.shape)


def update_kernel(rows_all, elements, *refs):
    part_ref, rows_ref, cols_ref, grad_ref, weights_ref = refs[:5]
    update_ref, new_ref, rows_out_ref, cols_out_ref = refs[5:]
    cols_out_ref[...] = cols_ref[...]
    summed = jnp.sum(part_ref[...], axis=0, keepdims=True)
    rows = to_column(rows_ref[...])
    for m in range(2):
        rows_out_ref[m:m + 1, :] = rows_ref[:, m * ROWS:(m + 1) * ROWS]
        ratio, rows_tot, weight = (summed[:, 2 * k + m:2 * k + m + 1] for k in range(3))
        mean_rows = rows_tot * (1.0 / rows_all)
        u_rms = jnp.sqrt(ratio * mean_rows * (1.0 / elements))
        w_rms = jnp.sqrt(weight * (1.0 / elements))
        factor = w_rms / jnp.maximum(1.0, u_rms)
        inverse = 1.0 / mean_rows
        here = rows[m * ROWS:(m + 1) * ROWS]
        for cols in chunks(grad_ref):
            second = here * cols_ref[m:m + 1, cols] * inverse
            step = grad_ref[m, :, cols] * lax.rsqrt(second) * factor
            update_ref[m, :, cols] = step
            new_ref[m, :, cols] = weights_ref[m, :, cols] - RATE * step


def pairing(first, kind):
    pairs = []
    for y in range(SIDE):
        for x in range(SIDE):
            for core in range(2):
                along_x = (core == 0) == first
                i = x if along_x else y
                j = (i ^ 1, SIDE - 1 - i, (i + 2) % SIDE)[kind]
                ny, nx = (y, j) if along_x else (j, x)
                pairs.append(((y * SIDE + x) * 2 + core, (ny * SIDE + nx) * 2 + core))
    return pairs


CORES = [(i, i ^ 1) for i in range(2 * SIDE * SIDE)]
PARTS = (((0, 2), (1, 3)), ((0, 1), (2, 3)))


def after(x, *earlier):
    return lax.optimization_barrier((x, *earlier))[0]


def body(activations, output_grads, token_counts, weights, row_state, col_state):
    ff_dev = output_grads.shape[2]
    rows_all = activations.shape[1]
    cols_all = ff_dev * lax.axis_size("mp")
    dp = lax.axis_index("dp")
    pos = jnp.stack([dp // (2 * SIDE), dp // 2 % SIDE, dp % 2]).astype(jnp.int32)
    turned = turn(pos, activations)
    tokens = activations.shape[0]
    half = ff_dev // 2
    quarter = SIDE * ROWS
    turned = turned.reshape(2, SIDE, quarter, tokens)

    def message(rows, i):
        return jax.ShapeDtypeStruct((rows + (EXTRA if i == 0 else 0), half), jnp.float32)

    pieces = 4
    got = [None] * pieces
    sent = [None] * pieces
    kept = [None] * pieces
    out = [None] * pieces

    def swap(i, *earlier):
        kernel = functools.partial(theirs_kernel, *divmod(i, 2))
        out[i] = call(kernel, message(SIDE * quarter, i), [VMEM] * 3)(after(turned, *earlier), token_counts, output_grads)
        got[i] = lax.ppermute(out[i], "dp", CORES)

    def first(i, *earlier):
        kernel = functools.partial(mine_kernel, *divmod(i, 2))
        sent[i], kept[i] = call(kernel, (message(2 * quarter, i),) * 2, [VMEM] * 4)(
            after(turned, *earlier), token_counts, output_grads, got[i]
        )
        got[i] = lax.ppermute(sent[i], "dp", pairing(True, i % 2))

    swap(0)
    for i in range(1, pieces):
        swap(i, out[i - 1])
    first(0, out[3])
    for i in range(1, pieces):
        first(i, sent[i - 1])
    last = sent[3]
    final = [None] * pieces
    for i in range(pieces):
        kernel = functools.partial(onward_kernel, quarter)
        last = call(kernel, message(quarter, i), [VMEM] * 2)(kept[i], after(got[i], last))
        final[i] = lax.ppermute(last, "dp", pairing(True, 1 - i % 2))
    share = jax.ShapeDtypeStruct((ROWS, ff_dev), jnp.float32)

    def deal(m):
        nonlocal last
        terms = [t for i in (2 * m, 2 * m + 1) for t in (kept[i], got[i], final[i])]
        terms[0] = after(terms[0], last)
        own, low, high, far = call(deal_kernel, (share,) * 4, [VMEM] * 6)(*terms)
        last = own
        far = lax.ppermute(far, "dp", pairing(False, 2))
        low = lax.ppermute(low, "dp", pairing(False, 0))
        high = lax.ppermute(high, "dp", pairing(False, 1))
        return own, low, high, far

    held = []
    for i in range(2):
        kernel = functools.partial(across_kernel, i)
        last, keep = call(kernel, (message(2 * ROWS, i),) * 2, [VMEM] * 3)(
            kept[i], got[i], after(final[i], last)
        )
        held.append([keep, lax.ppermute(last, "dp", pairing(False, i % 2))])
    for i in (0,):
        keep, came = held[i]
        kernel = functools.partial(onward_kernel, ROWS)
        last = call(kernel, message(ROWS, i), [VMEM] * 2)(keep, after(came, last))
        held[i].append(lax.ppermute(last, "dp", pairing(False, 1 - i % 2)))
    dealt = deal(1)
    for i in (1,):
        keep, came = held[i]
        kernel = functools.partial(onward_kernel, ROWS)
        last = call(kernel, message(ROWS, i), [VMEM] * 2)(keep, after(came, last))
        held[i].append(lax.ppermute(last, "dp", pairing(False, 1 - i % 2)))
    f32 = jnp.float32
    mine_shape = jax.ShapeDtypeStruct((2, ROWS, ff_dev), f32)
    lists = 2 * ff_dev // LANES
    dp_n, mp_n = lax.axis_size("dp"), lax.axis_size("mp")
    grad, part = call(
        columns_kernel,
        (mine_shape, jax.ShapeDtypeStruct((dp_n, lists, LANES), f32)),
        [VMEM] * 10,
    )(*held[0], *held[1], *dealt)
    part = lax.all_to_all(part, "dp", 0, 0, tiled=True)
    line = jax.ShapeDtypeStruct((1, LANES), f32)
    cols_new, part = call(
        functools.partial(rows_kernel, rows_all),
        (jax.ShapeDtypeStruct((2, ff_dev), f32), jax.ShapeDtypeStruct((mp_n, 4, LANES), f32)),
        [VMEM] * 4,
    )(part, grad, col_state, weights)
    part = lax.all_to_all(part, "mp", 0, 0, tiled=True)
    rows_new, part = call(
        functools.partial(totals_kernel, cols_all),
        (jax.ShapeDtypeStruct((1, LANES), f32), jax.ShapeDtypeStruct((dp_n, LANES), f32)),
        [VMEM] * 2,
    )(part, row_state)
    part = lax.all_to_all(part, "dp", 0, 0, tiled=True)
    rows_shape, cols_shape = (jax.ShapeDtypeStruct(t.shape, f32) for t in (row_state, col_state))
    return call(
        functools.partial(update_kernel, rows_all, rows_all * cols_all),
        (mine_shape, mine_shape, rows_shape, cols_shape),
        [VMEM] * 5,
    )(part, rows_new, cols_new, grad, weights)


def solution(mesh):
    in_specs = (
        P("dp", None),
        P(None, "dp", "mp"),
        P("dp", None),
        P(None, "dp", "mp"),
        P(None, "dp"),
        P(None, "mp"),
    )
    out_specs = (P(None, "dp", "mp"), P(None, "dp", "mp"), P(None, "dp"), P(None, "mp"))
    return jax.shard_map(body, mesh=mesh, in_specs=in_specs, out_specs=out_specs, check_vma=False)
```

```python
import functools

import jax
import jax.numpy as jnp
from jax import lax
from jax.experimental import pallas as pl
from jax.experimental.pallas import tpu as pltpu
from jax.sharding import PartitionSpec as P

DECAY = 1.0 - 4.0 ** (-0.8)
TINY = 1e-30
RATE = 0.01
SIDE = 4
ROWS = 64
BLOCK = 2 * ROWS
LANES = 128
SLOTS = 4
EXTRA = 8


def gray(i):
    return i ^ (i >> 1)


def turn_kernel(a_hbm, g_hbm, out_ref, g_ref, a_ref, sems):
    slot = a_ref.shape[0] // SLOTS

    def fetch(c):
        at = pl.ds(c * slot, slot)
        return pltpu.make_async_copy(a_hbm.at[at], a_ref.at[at], sems.at[c])

    for c in range(SLOTS):
        fetch(c).start()
    first = pltpu.make_async_copy(g_hbm.at[0], g_ref, sems.at[SLOTS])
    first.start()
    dp = lax.axis_index("dp")
    y, x, core = dp // (2 * SIDE), dp // 2 % SIDE, dp % 2
    places = []
    for by in range(SIDE):
        for bx in range(SIDE):
            rx = gray(x) ^ gray(bx)
            ry = gray(y) ^ gray(by)
            places.append((rx * SIDE + ry, ry * SIDE + rx))
    for c in range(SLOTS):
        fetch(c).wait()
        tokens = slice(c * slot, (c + 1) * slot)
        for k, (x_first, y_first) in enumerate(places):
            t = a_ref[tokens, k * BLOCK:(k + 1) * BLOCK].T
            out_ref[1 - core, x_first, :, tokens] = t[:ROWS]
            out_ref[core, y_first, :, tokens] = t[ROWS:]
    first.wait()


VMEM = pl.BlockSpec(memory_space=pltpu.VMEM)
FAR = pl.BlockSpec(memory_space=pltpu.HBM)
LIMIT = 24 * 1024 * 1024
TURN_LIMIT = 47 * 1024 * 1024
FIRST_LIMIT = 43 * 1024 * 1024


def call(kernel, out_shape, in_specs, flops=0, moved=0):
    several = isinstance(out_shape, tuple)
    return pl.pallas_call(
        kernel,
        out_shape=out_shape,
        in_specs=in_specs,
        out_specs=(VMEM,) * len(out_shape) if several else VMEM,
        cost_estimate=pl.CostEstimate(flops=flops, bytes_accessed=moved, transcendentals=0),
        compiler_params=pltpu.CompilerParams(vmem_limit_bytes=LIMIT),
    )


def turn(activations, output_grads):
    tokens, depth = activations.shape
    return pl.pallas_call(
        turn_kernel,
        out_shape=(
            jax.ShapeDtypeStruct((2, SIDE * SIDE, ROWS, tokens), activations.dtype),
            jax.ShapeDtypeStruct(output_grads.shape[1:], output_grads.dtype),
        ),
        in_specs=[FAR, FAR],
        out_specs=(VMEM, VMEM),
        scratch_shapes=[
            pltpu.VMEM((tokens, depth), activations.dtype),
            pltpu.SemaphoreType.DMA((SLOTS + 1,)),
        ],
        cost_estimate=pl.CostEstimate(flops=0, bytes_accessed=8 * 1024 * 1024, transcendentals=0),
        compiler_params=pltpu.CompilerParams(vmem_limit_bytes=TURN_LIMIT),
    )(activations, output_grads)


def live(counts_ref, tokens):
    width = tokens // SLOTS
    lane = lax.broadcasted_iota(jnp.int32, (1, tokens), 1)
    bound = jnp.zeros((1, tokens), jnp.int32)
    for b in range(SLOTS):
        bound = jnp.where(lane // width == b, counts_ref[:, b:b + 1] + b * width, bound)
    return jnp.where(lane < bound, 1.0, 0.0).astype(jnp.bfloat16)


def counted(counts_ref, out_ref):
    count = jnp.sum(counts_ref[...].astype(jnp.float32), axis=1, keepdims=True)
    return jnp.broadcast_to(count, (EXTRA, out_ref.shape[1]))


def theirs_kernel(piece, t_ref, counts_ref, g_ref, out_ref):
    half = out_ref.shape[1]
    quarter = t_ref.shape[2]
    g = g_ref[:, piece * half:(piece + 1) * half]
    mask = live(counts_ref, t_ref.shape[-1])
    for q in range(SIDE):
        left = t_ref[0, q] * mask
        rows = slice(q * quarter, (q + 1) * quarter)
        out_ref[rows] = jnp.dot(left, g, preferred_element_type=jnp.float32)
    if out_ref.shape[0] > SIDE * quarter:
        out_ref[SIDE * quarter:] = counted(counts_ref, out_ref)


def first_kernel(t_ref, counts_ref, g_ref, g_hbm, out_ref, next_ref, sem):
    copy = pltpu.make_async_copy(g_hbm.at[1], next_ref, sem)
    copy.start()
    theirs_kernel(0, t_ref, counts_ref, g_ref, out_ref)
    copy.wait()


def mine_kernel(piece, t_ref, counts_ref, g_ref, got_ref, send_ref, keep_ref):
    half = send_ref.shape[1]
    quarter = t_ref.shape[2]
    g = g_ref[:, piece * half:(piece + 1) * half]
    mask = live(counts_ref, t_ref.shape[-1])
    keep, send = PARTS[piece]
    for dst, order in ((send_ref, send), (keep_ref, keep)):
        for k, q in enumerate(order):
            left = t_ref[1, q] * mask
            came = got_ref[q * quarter:(q + 1) * quarter]
            product = jnp.dot(left, g, preferred_element_type=jnp.float32)
            dst[k * quarter:(k + 1) * quarter] = product + came
    if got_ref.shape[0] > SIDE * quarter:
        count = got_ref[SIDE * quarter:] + counted(counts_ref, got_ref)
        send_ref[2 * quarter:] = count
        keep_ref[2 * quarter:] = count


def onward_kernel(rows, keep_ref, got_ref, out_ref):
    out_ref[:rows] = keep_ref[rows:2 * rows] + got_ref[rows:2 * rows]
    if out_ref.shape[0] > rows:
        out_ref[rows:] = keep_ref[2 * rows:] + got_ref[2 * rows:]


def across_kernel(piece, kept_ref, got_ref, last_ref, send_ref, keep_ref):
    keep, send = PARTS[piece]
    for dst, order in ((send_ref, send), (keep_ref, keep)):
        for k, q in enumerate(order):
            rows = slice(q * ROWS, (q + 1) * ROWS)
            dst[k * ROWS:(k + 1) * ROWS] = kept_ref[rows] + got_ref[rows] + last_ref[rows]
    if send_ref.shape[0] > 2 * ROWS:
        count = kept_ref[-EXTRA:] + got_ref[-EXTRA:] + last_ref[-EXTRA:]
        send_ref[2 * ROWS:] = count
        keep_ref[2 * ROWS:] = count


def deal_kernel(*refs):
    outs = refs[6:]
    half = outs[0].shape[1] // 2
    for p in range(2):
        kept_ref, got_ref, last_ref = refs[3 * p:3 * p + 3]
        for q, out_ref in enumerate(outs):
            rows = slice(q * ROWS, (q + 1) * ROWS)
            out_ref[:, p * half:(p + 1) * half] = kept_ref[rows] + got_ref[rows] + last_ref[rows]


def chunks(ref):
    return [slice(k * LANES, (k + 1) * LANES) for k in range(ref.shape[-1] // LANES)]


def columns_kernel(*refs):
    grad_ref, part_ref = refs[10:]
    half = grad_ref.shape[2] // 2
    lists = grad_ref.shape[2] // LANES
    total = sum(ref[-EXTRA:][:1, :LANES] for ref in refs[:3])
    back = 1.0 / total

    def summed(m, k):
        if m == 1:
            own, low, high, far = (ref[:, k * LANES:(k + 1) * LANES] for ref in refs[6:10])
            return own + low + high + far
        piece, at = divmod(k * LANES, half)
        there = slice(at, at + LANES)
        kept, got, last = (ref[:ROWS, there] for ref in refs[3 * piece:3 * piece + 3])
        return kept + got + last

    for m in range(2):
        for k, cols in enumerate(chunks(grad_ref)):
            grad = summed(m, k) * back
            grad_ref[m, :, cols] = grad
            row = jnp.sum(grad * grad, axis=0, keepdims=True)
            part_ref[:, m * lists + k, :] = jnp.broadcast_to(row, (part_ref.shape[0], LANES))


def diagonal(n):
    shape = (n, n)
    return lax.broadcasted_iota(jnp.int32, shape, 0) == lax.broadcasted_iota(jnp.int32, shape, 1)


def to_row(column):
    return jnp.sum(jnp.where(diagonal(column.shape[0]), column, 0.0), axis=0, keepdims=True)


def to_column(row):
    return jnp.sum(jnp.where(diagonal(row.shape[1]), row, 0.0), axis=1, keepdims=True)


def rows_kernel(rows_all, part_ref, grad_ref, state_ref, weights_ref, cols_ref, out_ref):
    lists = grad_ref.shape[2] // LANES
    summed = jnp.sum(part_ref[...], axis=0)
    over, square, weight = [], [], []
    lane = lax.broadcasted_iota(jnp.int32, (1, LANES), 1)
    for m in range(2):
        zero = jnp.zeros((ROWS, LANES), jnp.float32)
        acc_over, acc_square, acc_weight = zero, zero, zero
        for k, cols in enumerate(chunks(grad_ref)):
            mean = summed[m * lists + k:m * lists + k + 1] * (1.0 / rows_all) + TINY
            new = DECAY * state_ref[m:m + 1, cols] + (1.0 - DECAY) * mean
            cols_ref[m:m + 1, cols] = new
            grad = grad_ref[m, :, cols]
            acc_square += grad * grad
            acc_over += grad * grad * (1.0 / new)
            w = weights_ref[m, :, cols]
            acc_weight += w * w
        over.append(jnp.sum(acc_over, axis=1, keepdims=True))
        square.append(jnp.sum(acc_square, axis=1, keepdims=True))
        both = jnp.sum(jnp.sum(acc_weight, axis=0, keepdims=True), axis=1, keepdims=True)
        weight.append(jnp.where(lane == m * ROWS, both, 0.0))
    lines = [to_row(jnp.concatenate(over, axis=0)), to_row(jnp.concatenate(square, axis=0))]
    lines.append(weight[0] + weight[1])
    for k in range(out_ref.shape[1]):
        line = lines[k] if k < len(lines) else jnp.zeros((1, LANES), jnp.float32)
        out_ref[:, k, :] = jnp.broadcast_to(line, (out_ref.shape[0], LANES))


def totals_kernel(cols_all, part_ref, state_ref, rows_ref, out_ref):
    summed = jnp.sum(part_ref[...], axis=0)
    state = to_row(jnp.concatenate([to_column(state_ref[m:m + 1]) for m in range(2)], axis=0))
    new = DECAY * state + (1.0 - DECAY) * (summed[1:2] * (1.0 / cols_all) + TINY)
    rows_ref[...] = new
    lane = lax.broadcasted_iota(jnp.int32, (1, LANES), 1)
    line = jnp.zeros((1, LANES), jnp.float32)
    for k, values in enumerate((summed[0:1] / new, new, summed[2:3])):
        for m in range(2):
            mine = (lane >= m * ROWS) & (lane < (m + 1) * ROWS)
            one = jnp.sum(jnp.where(mine, values, 0.0), axis=1, keepdims=True)
            line = jnp.where(lane == 2 * k + m, one, line)
    out_ref[...] = jnp.broadcast_to(line, out_ref.shape)


def update_kernel(rows_all, elements, *refs):
    part_ref, rows_ref, cols_ref, grad_ref, weights_ref = refs[:5]
    update_ref, new_ref, rows_out_ref, cols_out_ref = refs[5:]
    cols_out_ref[...] = cols_ref[...]
    summed = jnp.sum(part_ref[...], axis=0, keepdims=True)
    rows = to_column(rows_ref[...])
    for m in range(2):
        rows_out_ref[m:m + 1, :] = rows_ref[:, m * ROWS:(m + 1) * ROWS]
        ratio, rows_tot, weight = (summed[:, 2 * k + m:2 * k + m + 1] for k in range(3))
        mean_rows = rows_tot * (1.0 / rows_all)
        u_rms = jnp.sqrt(ratio * mean_rows * (1.0 / elements))
        w_rms = jnp.sqrt(weight * (1.0 / elements))
        factor = w_rms / jnp.maximum(1.0, u_rms)
        inverse = 1.0 / mean_rows
        here = rows[m * ROWS:(m + 1) * ROWS]
        for cols in chunks(grad_ref):
            second = here * cols_ref[m:m + 1, cols] * inverse
            step = grad_ref[m, :, cols] * lax.rsqrt(second) * factor
            update_ref[m, :, cols] = step
            new_ref[m, :, cols] = weights_ref[m, :, cols] - RATE * step


def pairing(first, kind):
    pairs = []
    for y in range(SIDE):
        for x in range(SIDE):
            for core in range(2):
                along_x = (core == 0) == first
                i = x if along_x else y
                j = (i ^ 1, SIDE - 1 - i, (i + 2) % SIDE)[kind]
                ny, nx = (y, j) if along_x else (j, x)
                pairs.append(((y * SIDE + x) * 2 + core, (ny * SIDE + nx) * 2 + core))
    return pairs


CORES = [(i, i ^ 1) for i in range(2 * SIDE * SIDE)]
PARTS = (((0, 2), (1, 3)), ((0, 1), (2, 3)))


def after(x, *earlier):
    return lax.optimization_barrier((x, *earlier))[0]


def body(activations, output_grads, token_counts, weights, row_state, col_state):
    ff_dev = output_grads.shape[2]
    rows_all = activations.shape[1]
    cols_all = ff_dev * lax.axis_size("mp")
    turned, first_grads = turn(activations, output_grads)
    tokens = activations.shape[0]
    half = ff_dev // 2
    quarter = SIDE * ROWS
    turned = turned.reshape(2, SIDE, quarter, tokens)

    def message(rows, i):
        return jax.ShapeDtypeStruct((rows + (EXTRA if i == 0 else 0), half), jnp.float32)

    pieces = 4
    got = [None] * pieces
    sent = [None] * pieces
    kept = [None] * pieces
    out = [None] * pieces

    grads = [first_grads, None]

    def swap(i, *earlier):
        if i == 0:
            out[0], grads[1] = pl.pallas_call(
                first_kernel,
                out_shape=(message(SIDE * quarter, 0), jax.ShapeDtypeStruct(first_grads.shape, first_grads.dtype)),
                in_specs=[VMEM, VMEM, VMEM, FAR],
                out_specs=(VMEM, VMEM),
                scratch_shapes=[pltpu.SemaphoreType.DMA],
                cost_estimate=pl.CostEstimate(flops=0, bytes_accessed=0, transcendentals=0),
                compiler_params=pltpu.CompilerParams(vmem_limit_bytes=FIRST_LIMIT),
            )(turned, token_counts, first_grads, output_grads)
        else:
            kernel = functools.partial(theirs_kernel, i % 2)
            out[i] = call(kernel, message(SIDE * quarter, i), [VMEM] * 3)(
                after(turned, *earlier), token_counts, grads[i // 2]
            )
        got[i] = lax.ppermute(out[i], "dp", CORES)

    def first(i, *earlier):
        kernel = functools.partial(mine_kernel, i % 2)
        sent[i], kept[i] = call(kernel, (message(2 * quarter, i),) * 2, [VMEM] * 4)(
            after(turned, *earlier), token_counts, grads[i // 2], got[i]
        )
        got[i] = lax.ppermute(sent[i], "dp", pairing(True, i % 2))

    swap(0)
    for i in range(1, pieces):
        swap(i, out[i - 1])
    first(0, out[3])
    for i in range(1, pieces):
        first(i, sent[i - 1])
    last = sent[3]
    final = [None] * pieces
    for i in range(pieces):
        kernel = functools.partial(onward_kernel, quarter)
        last = call(kernel, message(quarter, i), [VMEM] * 2)(kept[i], after(got[i], last))
        final[i] = lax.ppermute(last, "dp", pairing(True, 1 - i % 2))
    share = jax.ShapeDtypeStruct((ROWS, ff_dev), jnp.float32)

    def deal(m):
        nonlocal last
        terms = [t for i in (2 * m, 2 * m + 1) for t in (kept[i], got[i], final[i])]
        terms[0] = after(terms[0], last)
        own, low, high, far = call(deal_kernel, (share,) * 4, [VMEM] * 6)(*terms)
        last = own
        low = lax.ppermute(low, "dp", pairing(False, 0))
        high = lax.ppermute(high, "dp", pairing(False, 1))
        far = lax.ppermute(far, "dp", pairing(False, 2))
        return own, low, high, far

    held = []
    for i in range(2):
        kernel = functools.partial(across_kernel, i)
        last, keep = call(kernel, (message(2 * ROWS, i),) * 2, [VMEM] * 3)(
            kept[i], got[i], after(final[i], last)
        )
        held.append([keep, lax.ppermute(last, "dp", pairing(False, i % 2))])
    for i in (0,):
        keep, came = held[i]
        kernel = functools.partial(onward_kernel, ROWS)
        last = call(kernel, message(ROWS, i), [VMEM] * 2)(keep, after(came, last))
        held[i].append(lax.ppermute(last, "dp", pairing(False, 1 - i % 2)))
    dealt = deal(1)
    for i in (1,):
        keep, came = held[i]
        kernel = functools.partial(onward_kernel, ROWS)
        last = call(kernel, message(ROWS, i), [VMEM] * 2)(keep, after(came, last))
        held[i].append(lax.ppermute(last, "dp", pairing(False, 1 - i % 2)))
    f32 = jnp.float32
    mine_shape = jax.ShapeDtypeStruct((2, ROWS, ff_dev), f32)
    lists = 2 * ff_dev // LANES
    dp_n, mp_n = lax.axis_size("dp"), lax.axis_size("mp")
    grad, part = call(
        columns_kernel,
        (mine_shape, jax.ShapeDtypeStruct((dp_n, lists, LANES), f32)),
        [VMEM] * 10,
    )(*held[0], *held[1], *dealt)
    part = lax.all_to_all(part, "dp", 0, 0, tiled=True)
    line = jax.ShapeDtypeStruct((1, LANES), f32)
    cols_new, part = call(
        functools.partial(rows_kernel, rows_all),
        (jax.ShapeDtypeStruct((2, ff_dev), f32), jax.ShapeDtypeStruct((mp_n, 4, LANES), f32)),
        [VMEM] * 4,
    )(part, grad, col_state, weights)
    part = lax.all_to_all(part, "mp", 0, 0, tiled=True)
    rows_new, part = call(
        functools.partial(totals_kernel, cols_all),
        (jax.ShapeDtypeStruct((1, LANES), f32), jax.ShapeDtypeStruct((dp_n, LANES), f32)),
        [VMEM] * 2,
    )(part, row_state)
    part = lax.all_to_all(part, "dp", 0, 0, tiled=True)
    rows_shape, cols_shape = (jax.ShapeDtypeStruct(t.shape, f32) for t in (row_state, col_state))
    return call(
        functools.partial(update_kernel, rows_all, rows_all * cols_all),
        (mine_shape, mine_shape, rows_shape, cols_shape),
        [VMEM] * 5,
    )(part, rows_new, cols_new, grad, weights)


def solution(mesh):
    in_specs = (
        P("dp", None),
        P(None, "dp", "mp"),
        P("dp", None),
        P(None, "dp", "mp"),
        P(None, "dp"),
        P(None, "mp"),
    )
    out_specs = (P(None, "dp", "mp"), P(None, "dp", "mp"), P(None, "dp"), P(None, "mp"))
    return jax.shard_map(body, mesh=mesh, in_specs=in_specs, out_specs=out_specs, check_vma=False)
```

```python
import functools

import jax
import jax.numpy as jnp
from jax import lax
from jax.experimental import pallas as pl
from jax.experimental.pallas import tpu as pltpu
from jax.sharding import PartitionSpec as P

DECAY = 1.0 - 4.0 ** (-0.8)
TINY = 1e-30
RATE = 0.01
SIDE = 4
ROWS = 64
BLOCK = 2 * ROWS
LANES = 128
SLOTS = 4
EXTRA = 8


def gray(i):
    return i ^ (i >> 1)


def turn_kernel(a_hbm, g_hbm, out_ref, g_ref, a_ref, sems):
    slot = a_ref.shape[0] // SLOTS

    def fetch(c):
        at = pl.ds(c * slot, slot)
        return pltpu.make_async_copy(a_hbm.at[at], a_ref.at[at], sems.at[c])

    for c in range(SLOTS):
        fetch(c).start()
    first = pltpu.make_async_copy(g_hbm.at[0], g_ref, sems.at[SLOTS])
    first.start()
    dp = lax.axis_index("dp")
    y, x, core = dp // (2 * SIDE), dp // 2 % SIDE, dp % 2
    places = []
    for by in range(SIDE):
        for bx in range(SIDE):
            rx = gray(x) ^ gray(bx)
            ry = gray(y) ^ gray(by)
            places.append((rx * SIDE + ry, ry * SIDE + rx))
    for c in range(SLOTS):
        fetch(c).wait()
        tokens = slice(c * slot, (c + 1) * slot)
        for k, (x_first, y_first) in enumerate(places):
            t = a_ref[tokens, k * BLOCK:(k + 1) * BLOCK].T
            out_ref[1 - core, x_first, :, tokens] = t[:ROWS]
            out_ref[core, y_first, :, tokens] = t[ROWS:]
    first.wait()


VMEM = pl.BlockSpec(memory_space=pltpu.VMEM)
FAR = pl.BlockSpec(memory_space=pltpu.HBM)
LIMIT = 24 * 1024 * 1024
TURN_LIMIT = 47 * 1024 * 1024
FIRST_LIMIT = 43 * 1024 * 1024


def call(kernel, out_shape, in_specs, flops=0, moved=0):
    several = isinstance(out_shape, tuple)
    return pl.pallas_call(
        kernel,
        out_shape=out_shape,
        in_specs=in_specs,
        out_specs=(VMEM,) * len(out_shape) if several else VMEM,
        cost_estimate=pl.CostEstimate(flops=flops, bytes_accessed=moved, transcendentals=0),
        compiler_params=pltpu.CompilerParams(vmem_limit_bytes=LIMIT),
    )


def turn(activations, output_grads):
    tokens, depth = activations.shape
    return pl.pallas_call(
        turn_kernel,
        out_shape=(
            jax.ShapeDtypeStruct((2, SIDE * SIDE, ROWS, tokens), activations.dtype),
            jax.ShapeDtypeStruct(output_grads.shape[1:], output_grads.dtype),
        ),
        in_specs=[FAR, FAR],
        out_specs=(VMEM, VMEM),
        scratch_shapes=[
            pltpu.VMEM((tokens, depth), activations.dtype),
            pltpu.SemaphoreType.DMA((SLOTS + 1,)),
        ],
        cost_estimate=pl.CostEstimate(flops=0, bytes_accessed=8 * 1024 * 1024, transcendentals=0),
        compiler_params=pltpu.CompilerParams(vmem_limit_bytes=TURN_LIMIT),
    )(activations, output_grads)


def live(counts_ref, tokens):
    width = tokens // SLOTS
    lane = lax.broadcasted_iota(jnp.int32, (1, tokens), 1)
    bound = jnp.zeros((1, tokens), jnp.int32)
    for b in range(SLOTS):
        bound = jnp.where(lane // width == b, counts_ref[:, b:b + 1] + b * width, bound)
    return jnp.where(lane < bound, 1.0, 0.0).astype(jnp.bfloat16)


def counted(counts_ref, out_ref):
    count = jnp.sum(counts_ref[...].astype(jnp.float32), axis=1, keepdims=True)
    return jnp.broadcast_to(count, (EXTRA, out_ref.shape[1]))


def theirs_kernel(piece, t_ref, counts_ref, g_ref, out_ref):
    half = out_ref.shape[1]
    quarter = t_ref.shape[2]
    g = g_ref[:, piece * half:(piece + 1) * half]
    mask = live(counts_ref, t_ref.shape[-1])
    for q in range(SIDE):
        left = t_ref[0, q] * mask
        rows = slice(q * quarter, (q + 1) * quarter)
        out_ref[rows] = jnp.dot(left, g, preferred_element_type=jnp.float32)
    if out_ref.shape[0] > SIDE * quarter:
        out_ref[SIDE * quarter:] = counted(counts_ref, out_ref)


def first_kernel(t_ref, counts_ref, g_ref, g_hbm, out_ref, next_ref, sem):
    copy = pltpu.make_async_copy(g_hbm.at[1], next_ref, sem)
    copy.start()
    theirs_kernel(0, t_ref, counts_ref, g_ref, out_ref)
    copy.wait()


def mine_kernel(piece, which, t_ref, counts_ref, g_ref, got_ref, out_ref):
    half = out_ref.shape[1]
    quarter = t_ref.shape[2]
    g = g_ref[:, piece * half:(piece + 1) * half]
    mask = live(counts_ref, t_ref.shape[-1])
    for k, q in enumerate(PARTS[piece][which]):
        left = t_ref[1, q] * mask
        came = got_ref[q * quarter:(q + 1) * quarter]
        product = jnp.dot(left, g, preferred_element_type=jnp.float32)
        out_ref[k * quarter:(k + 1) * quarter] = product + came
    if got_ref.shape[0] > SIDE * quarter:
        out_ref[2 * quarter:] = got_ref[SIDE * quarter:] + counted(counts_ref, got_ref)


def onward_kernel(rows, keep_ref, got_ref, out_ref):
    out_ref[:rows] = keep_ref[rows:2 * rows] + got_ref[rows:2 * rows]
    if out_ref.shape[0] > rows:
        out_ref[rows:] = keep_ref[2 * rows:] + got_ref[2 * rows:]


def across_kernel(piece, kept_ref, got_ref, last_ref, send_ref, keep_ref):
    keep, send = PARTS[piece]
    for dst, order in ((send_ref, send), (keep_ref, keep)):
        for k, q in enumerate(order):
            rows = slice(q * ROWS, (q + 1) * ROWS)
            dst[k * ROWS:(k + 1) * ROWS] = kept_ref[rows] + got_ref[rows] + last_ref[rows]
    if send_ref.shape[0] > 2 * ROWS:
        count = kept_ref[-EXTRA:] + got_ref[-EXTRA:] + last_ref[-EXTRA:]
        send_ref[2 * ROWS:] = count
        keep_ref[2 * ROWS:] = count


def deal_kernel(*refs):
    outs = refs[6:]
    half = outs[0].shape[1] // 2
    for p in range(2):
        kept_ref, got_ref, last_ref = refs[3 * p:3 * p + 3]
        for q, out_ref in enumerate(outs):
            rows = slice(q * ROWS, (q + 1) * ROWS)
            out_ref[:, p * half:(p + 1) * half] = kept_ref[rows] + got_ref[rows] + last_ref[rows]


def chunks(ref):
    return [slice(k * LANES, (k + 1) * LANES) for k in range(ref.shape[-1] // LANES)]


def columns_kernel(*refs):
    grad_ref, part_ref = refs[10:]
    half = grad_ref.shape[2] // 2
    lists = grad_ref.shape[2] // LANES
    total = sum(ref[-EXTRA:][:1, :LANES] for ref in refs[:3])
    back = 1.0 / total

    def summed(m, k):
        if m == 1:
            own, low, high, far = (ref[:, k * LANES:(k + 1) * LANES] for ref in refs[6:10])
            return own + low + high + far
        piece, at = divmod(k * LANES, half)
        there = slice(at, at + LANES)
        kept, got, last = (ref[:ROWS, there] for ref in refs[3 * piece:3 * piece + 3])
        return kept + got + last

    for m in range(2):
        for k, cols in enumerate(chunks(grad_ref)):
            grad = summed(m, k) * back
            grad_ref[m, :, cols] = grad
            row = jnp.sum(grad * grad, axis=0, keepdims=True)
            part_ref[:, m * lists + k, :] = jnp.broadcast_to(row, (part_ref.shape[0], LANES))


def diagonal(n):
    shape = (n, n)
    return lax.broadcasted_iota(jnp.int32, shape, 0) == lax.broadcasted_iota(jnp.int32, shape, 1)


def to_row(column):
    return jnp.sum(jnp.where(diagonal(column.shape[0]), column, 0.0), axis=0, keepdims=True)


def to_column(row):
    return jnp.sum(jnp.where(diagonal(row.shape[1]), row, 0.0), axis=1, keepdims=True)


def rows_kernel(rows_all, part_ref, grad_ref, state_ref, weights_ref, cols_ref, out_ref):
    lists = grad_ref.shape[2] // LANES
    summed = jnp.sum(part_ref[...], axis=0)
    over, square, weight = [], [], []
    lane = lax.broadcasted_iota(jnp.int32, (1, LANES), 1)
    for m in range(2):
        zero = jnp.zeros((ROWS, LANES), jnp.float32)
        acc_over, acc_square, acc_weight = zero, zero, zero
        for k, cols in enumerate(chunks(grad_ref)):
            mean = summed[m * lists + k:m * lists + k + 1] * (1.0 / rows_all) + TINY
            new = DECAY * state_ref[m:m + 1, cols] + (1.0 - DECAY) * mean
            cols_ref[m:m + 1, cols] = new
            grad = grad_ref[m, :, cols]
            acc_square += grad * grad
            acc_over += grad * grad * (1.0 / new)
            w = weights_ref[m, :, cols]
            acc_weight += w * w
        over.append(jnp.sum(acc_over, axis=1, keepdims=True))
        square.append(jnp.sum(acc_square, axis=1, keepdims=True))
        both = jnp.sum(jnp.sum(acc_weight, axis=0, keepdims=True), axis=1, keepdims=True)
        weight.append(jnp.where(lane == m * ROWS, both, 0.0))
    lines = [to_row(jnp.concatenate(over, axis=0)), to_row(jnp.concatenate(square, axis=0))]
    lines.append(weight[0] + weight[1])
    for k in range(out_ref.shape[1]):
        line = lines[k] if k < len(lines) else jnp.zeros((1, LANES), jnp.float32)
        out_ref[:, k, :] = jnp.broadcast_to(line, (out_ref.shape[0], LANES))


def totals_kernel(cols_all, part_ref, state_ref, rows_ref, out_ref):
    summed = jnp.sum(part_ref[...], axis=0)
    state = to_row(jnp.concatenate([to_column(state_ref[m:m + 1]) for m in range(2)], axis=0))
    new = DECAY * state + (1.0 - DECAY) * (summed[1:2] * (1.0 / cols_all) + TINY)
    rows_ref[...] = new
    lane = lax.broadcasted_iota(jnp.int32, (1, LANES), 1)
    line = jnp.zeros((1, LANES), jnp.float32)
    for k, values in enumerate((summed[0:1] / new, new, summed[2:3])):
        for m in range(2):
            mine = (lane >= m * ROWS) & (lane < (m + 1) * ROWS)
            one = jnp.sum(jnp.where(mine, values, 0.0), axis=1, keepdims=True)
            line = jnp.where(lane == 2 * k + m, one, line)
    out_ref[...] = jnp.broadcast_to(line, out_ref.shape)


def update_kernel(rows_all, elements, *refs):
    part_ref, rows_ref, cols_ref, grad_ref, weights_ref = refs[:5]
    update_ref, new_ref, rows_out_ref, cols_out_ref = refs[5:]
    cols_out_ref[...] = cols_ref[...]
    summed = jnp.sum(part_ref[...], axis=0, keepdims=True)
    rows = to_column(rows_ref[...])
    for m in range(2):
        rows_out_ref[m:m + 1, :] = rows_ref[:, m * ROWS:(m + 1) * ROWS]
        ratio, rows_tot, weight = (summed[:, 2 * k + m:2 * k + m + 1] for k in range(3))
        mean_rows = rows_tot * (1.0 / rows_all)
        u_rms = jnp.sqrt(ratio * mean_rows * (1.0 / elements))
        w_rms = jnp.sqrt(weight * (1.0 / elements))
        factor = w_rms / jnp.maximum(1.0, u_rms)
        inverse = 1.0 / mean_rows
        here = rows[m * ROWS:(m + 1) * ROWS]
        for cols in chunks(grad_ref):
            second = here * cols_ref[m:m + 1, cols] * inverse
            step = grad_ref[m, :, cols] * lax.rsqrt(second) * factor
            update_ref[m, :, cols] = step
            new_ref[m, :, cols] = weights_ref[m, :, cols] - RATE * step


def pairing(first, kind):
    pairs = []
    for y in range(SIDE):
        for x in range(SIDE):
            for core in range(2):
                along_x = (core == 0) == first
                i = x if along_x else y
                j = (i ^ 1, SIDE - 1 - i, (i + 2) % SIDE)[kind]
                ny, nx = (y, j) if along_x else (j, x)
                pairs.append(((y * SIDE + x) * 2 + core, (ny * SIDE + nx) * 2 + core))
    return pairs


CORES = [(i, i ^ 1) for i in range(2 * SIDE * SIDE)]
PARTS = (((0, 2), (1, 3)), ((0, 1), (2, 3)))


def after(x, *earlier):
    return lax.optimization_barrier((x, *earlier))[0]


def body(activations, output_grads, token_counts, weights, row_state, col_state):
    ff_dev = output_grads.shape[2]
    rows_all = activations.shape[1]
    cols_all = ff_dev * lax.axis_size("mp")
    turned, first_grads = turn(activations, output_grads)
    tokens = activations.shape[0]
    half = ff_dev // 2
    quarter = SIDE * ROWS
    turned = turned.reshape(2, SIDE, quarter, tokens)

    def message(rows, i):
        return jax.ShapeDtypeStruct((rows + (EXTRA if i == 0 else 0), half), jnp.float32)

    pieces = 4
    got = [None] * pieces
    sent = [None] * pieces
    kept = [None] * pieces
    out = [None] * pieces

    grads = [first_grads, None]

    def swap(i, *earlier):
        if i == 0:
            out[0], grads[1] = pl.pallas_call(
                first_kernel,
                out_shape=(message(SIDE * quarter, 0), jax.ShapeDtypeStruct(first_grads.shape, first_grads.dtype)),
                in_specs=[VMEM, VMEM, VMEM, FAR],
                out_specs=(VMEM, VMEM),
                scratch_shapes=[pltpu.SemaphoreType.DMA],
                cost_estimate=pl.CostEstimate(flops=0, bytes_accessed=0, transcendentals=0),
                compiler_params=pltpu.CompilerParams(vmem_limit_bytes=FIRST_LIMIT),
            )(turned, token_counts, first_grads, output_grads)
        else:
            kernel = functools.partial(theirs_kernel, i % 2)
            out[i] = call(kernel, message(SIDE * quarter, i), [VMEM] * 3)(
                after(turned, *earlier), token_counts, grads[i // 2]
            )
        got[i] = lax.ppermute(out[i], "dp", CORES)

    def share_of(i, which, came, *earlier):
        kernel = functools.partial(mine_kernel, i % 2, which)
        return call(kernel, message(2 * quarter, i), [VMEM] * 4)(
            after(turned, *earlier), token_counts, grads[i // 2], came
        )

    swapped = [None] * pieces

    def first(i, *earlier):
        swapped[i] = got[i]
        sent[i] = share_of(i, 1, swapped[i], *earlier)
        got[i] = lax.ppermute(sent[i], "dp", pairing(True, i % 2))

    swap(0)
    for i in range(1, pieces):
        swap(i, out[i - 1])
    first(0, out[3])
    for i in range(1, pieces):
        first(i, sent[i - 1])
    last = sent[3]
    for i in range(pieces):
        last = kept[i] = share_of(i, 0, swapped[i], last)
    final = [None] * pieces
    for i in range(pieces):
        kernel = functools.partial(onward_kernel, quarter)
        last = call(kernel, message(quarter, i), [VMEM] * 2)(kept[i], after(got[i], last))
        final[i] = lax.ppermute(last, "dp", pairing(True, 1 - i % 2))
    share = jax.ShapeDtypeStruct((ROWS, ff_dev), jnp.float32)

    def deal(m):
        nonlocal last
        terms = [t for i in (2 * m, 2 * m + 1) for t in (kept[i], got[i], final[i])]
        terms[0] = after(terms[0], last)
        own, low, high, far = call(deal_kernel, (share,) * 4, [VMEM] * 6)(*terms)
        last = own
        low = lax.ppermute(low, "dp", pairing(False, 0))
        high = lax.ppermute(high, "dp", pairing(False, 1))
        far = lax.ppermute(far, "dp", pairing(False, 2))
        return own, low, high, far

    held = []
    for i in range(2):
        kernel = functools.partial(across_kernel, i)
        last, keep = call(kernel, (message(2 * ROWS, i),) * 2, [VMEM] * 3)(
            kept[i], got[i], after(final[i], last)
        )
        held.append([keep, lax.ppermute(last, "dp", pairing(False, i % 2))])
    for i in (0,):
        keep, came = held[i]
        kernel = functools.partial(onward_kernel, ROWS)
        last = call(kernel, message(ROWS, i), [VMEM] * 2)(keep, after(came, last))
        held[i].append(lax.ppermute(last, "dp", pairing(False, 1 - i % 2)))
    dealt = deal(1)
    for i in (1,):
        keep, came = held[i]
        kernel = functools.partial(onward_kernel, ROWS)
        last = call(kernel, message(ROWS, i), [VMEM] * 2)(keep, after(came, last))
        held[i].append(lax.ppermute(last, "dp", pairing(False, 1 - i % 2)))
    f32 = jnp.float32
    mine_shape = jax.ShapeDtypeStruct((2, ROWS, ff_dev), f32)
    lists = 2 * ff_dev // LANES
    dp_n, mp_n = lax.axis_size("dp"), lax.axis_size("mp")
    grad, part = call(
        columns_kernel,
        (mine_shape, jax.ShapeDtypeStruct((dp_n, lists, LANES), f32)),
        [VMEM] * 10,
    )(*held[0], *held[1], *dealt)
    part = lax.all_to_all(part, "dp", 0, 0, tiled=True)
    line = jax.ShapeDtypeStruct((1, LANES), f32)
    cols_new, part = call(
        functools.partial(rows_kernel, rows_all),
        (jax.ShapeDtypeStruct((2, ff_dev), f32), jax.ShapeDtypeStruct((mp_n, 4, LANES), f32)),
        [VMEM] * 4,
    )(part, grad, col_state, weights)
    part = lax.all_to_all(part, "mp", 0, 0, tiled=True)
    rows_new, part = call(
        functools.partial(totals_kernel, cols_all),
        (jax.ShapeDtypeStruct((1, LANES), f32), jax.ShapeDtypeStruct((dp_n, LANES), f32)),
        [VMEM] * 2,
    )(part, row_state)
    part = lax.all_to_all(part, "dp", 0, 0, tiled=True)
    rows_shape, cols_shape = (jax.ShapeDtypeStruct(t.shape, f32) for t in (row_state, col_state))
    return call(
        functools.partial(update_kernel, rows_all, rows_all * cols_all),
        (mine_shape, mine_shape, rows_shape, cols_shape),
        [VMEM] * 5,
    )(part, rows_new, cols_new, grad, weights)


def solution(mesh):
    in_specs = (
        P("dp", None),
        P(None, "dp", "mp"),
        P("dp", None),
        P(None, "dp", "mp"),
        P(None, "dp"),
        P(None, "mp"),
    )
    out_specs = (P(None, "dp", "mp"), P(None, "dp", "mp"), P(None, "dp"), P(None, "mp"))
    return jax.shard_map(body, mesh=mesh, in_specs=in_specs, out_specs=out_specs, check_vma=False)
```

```python
import functools

import jax
import jax.numpy as jnp
from jax import lax
from jax.experimental import pallas as pl
from jax.experimental.pallas import tpu as pltpu
from jax.sharding import PartitionSpec as P

DECAY = 1.0 - 4.0 ** (-0.8)
TINY = 1e-30
RATE = 0.01
SIDE = 4
ROWS = 64
BLOCK = 2 * ROWS
LANES = 128
SLOTS = 4
EXTRA = 8


def gray(i):
    return i ^ (i >> 1)


def turn_kernel(a_hbm, g_hbm, out_ref, g_ref, a_ref, sems):
    slot = a_ref.shape[0] // SLOTS

    def fetch(c):
        at = pl.ds(c * slot, slot)
        return pltpu.make_async_copy(a_hbm.at[at], a_ref.at[at], sems.at[c])

    for c in range(SLOTS):
        fetch(c).start()
    first = pltpu.make_async_copy(g_hbm.at[0], g_ref, sems.at[SLOTS])
    first.start()
    dp = lax.axis_index("dp")
    y, x, core = dp // (2 * SIDE), dp // 2 % SIDE, dp % 2
    places = []
    for by in range(SIDE):
        for bx in range(SIDE):
            rx = gray(x) ^ gray(bx)
            ry = gray(y) ^ gray(by)
            places.append((rx * SIDE + ry, ry * SIDE + rx))
    for c in range(SLOTS):
        fetch(c).wait()
        tokens = slice(c * slot, (c + 1) * slot)
        for k, (x_first, y_first) in enumerate(places):
            t = a_ref[tokens, k * BLOCK:(k + 1) * BLOCK].T
            out_ref[1 - core, x_first, :, tokens] = t[:ROWS]
            out_ref[core, y_first, :, tokens] = t[ROWS:]
    first.wait()


VMEM = pl.BlockSpec(memory_space=pltpu.VMEM)
FAR = pl.BlockSpec(memory_space=pltpu.HBM)
LIMIT = 24 * 1024 * 1024
TURN_LIMIT = 47 * 1024 * 1024
FIRST_LIMIT = 39 * 1024 * 1024


def call(kernel, out_shape, in_specs, flops=0, moved=0):
    several = isinstance(out_shape, tuple)
    return pl.pallas_call(
        kernel,
        out_shape=out_shape,
        in_specs=in_specs,
        out_specs=(VMEM,) * len(out_shape) if several else VMEM,
        cost_estimate=pl.CostEstimate(flops=flops, bytes_accessed=moved, transcendentals=0),
        compiler_params=pltpu.CompilerParams(vmem_limit_bytes=LIMIT),
    )


def turn(activations, output_grads):
    tokens, depth = activations.shape
    return pl.pallas_call(
        turn_kernel,
        out_shape=(
            jax.ShapeDtypeStruct((2, SIDE * SIDE, ROWS, tokens), activations.dtype),
            jax.ShapeDtypeStruct(output_grads.shape[1:], output_grads.dtype),
        ),
        in_specs=[FAR, FAR],
        out_specs=(VMEM, VMEM),
        scratch_shapes=[
            pltpu.VMEM((tokens, depth), activations.dtype),
            pltpu.SemaphoreType.DMA((SLOTS + 1,)),
        ],
        cost_estimate=pl.CostEstimate(flops=0, bytes_accessed=8 * 1024 * 1024, transcendentals=0),
        compiler_params=pltpu.CompilerParams(vmem_limit_bytes=TURN_LIMIT),
    )(activations, output_grads)


def live(counts_ref, tokens):
    width = tokens // SLOTS
    lane = lax.broadcasted_iota(jnp.int32, (1, tokens), 1)
    bound = jnp.zeros((1, tokens), jnp.int32)
    for b in range(SLOTS):
        bound = jnp.where(lane // width == b, counts_ref[:, b:b + 1] + b * width, bound)
    return jnp.where(lane < bound, 1.0, 0.0).astype(jnp.bfloat16)


def counted(counts_ref, out_ref):
    count = jnp.sum(counts_ref[...].astype(jnp.float32), axis=1, keepdims=True)
    return jnp.broadcast_to(count, (EXTRA, out_ref.shape[1]))


def theirs_kernel(piece, t_ref, counts_ref, g_ref, out_ref):
    half = out_ref.shape[1]
    quarter = t_ref.shape[2]
    g = g_ref[:, piece * half:(piece + 1) * half]
    mask = live(counts_ref, t_ref.shape[-1])
    for q in range(SIDE):
        left = t_ref[0, q] * mask
        rows = slice(q * quarter, (q + 1) * quarter)
        out_ref[rows] = jnp.dot(left, g, preferred_element_type=jnp.float32)
    if out_ref.shape[0] > SIDE * quarter:
        out_ref[SIDE * quarter:] = counted(counts_ref, out_ref)


def first_kernel(t_ref, counts_ref, g_ref, g_hbm, out_ref, next_ref, sem):
    copy = pltpu.make_async_copy(g_hbm.at[1], next_ref, sem)
    copy.start()
    theirs_kernel(1, t_ref, counts_ref, g_ref, out_ref)
    copy.wait()


def mine_kernel(piece, which, t_ref, counts_ref, g_ref, got_ref, out_ref):
    half = out_ref.shape[1]
    quarter = t_ref.shape[2]
    g = g_ref[:, piece * half:(piece + 1) * half]
    mask = live(counts_ref, t_ref.shape[-1])
    for k, q in enumerate(PARTS[piece][which]):
        left = t_ref[1, q] * mask
        came = got_ref[q * quarter:(q + 1) * quarter]
        product = jnp.dot(left, g, preferred_element_type=jnp.float32)
        out_ref[k * quarter:(k + 1) * quarter] = product + came
    if got_ref.shape[0] > SIDE * quarter:
        out_ref[2 * quarter:] = got_ref[SIDE * quarter:] + counted(counts_ref, got_ref)


def onward_kernel(rows, keep_ref, got_ref, out_ref):
    out_ref[:rows] = keep_ref[rows:2 * rows] + got_ref[rows:2 * rows]
    if out_ref.shape[0] > rows:
        out_ref[rows:] = keep_ref[2 * rows:] + got_ref[2 * rows:]


def across_kernel(piece, kept_ref, got_ref, last_ref, send_ref, keep_ref):
    keep, send = PARTS[piece]
    for dst, order in ((send_ref, send), (keep_ref, keep)):
        for k, q in enumerate(order):
            rows = slice(q * ROWS, (q + 1) * ROWS)
            dst[k * ROWS:(k + 1) * ROWS] = kept_ref[rows] + got_ref[rows] + last_ref[rows]
    if send_ref.shape[0] > 2 * ROWS:
        count = kept_ref[-EXTRA:] + got_ref[-EXTRA:] + last_ref[-EXTRA:]
        send_ref[2 * ROWS:] = count
        keep_ref[2 * ROWS:] = count


def deal_kernel(*refs):
    outs = refs[6:]
    half = outs[0].shape[1] // 2
    for p in range(2):
        kept_ref, got_ref, last_ref = refs[3 * p:3 * p + 3]
        for q, out_ref in enumerate(outs):
            rows = slice(q * ROWS, (q + 1) * ROWS)
            out_ref[:, p * half:(p + 1) * half] = kept_ref[rows] + got_ref[rows] + last_ref[rows]


def chunks(ref):
    return [slice(k * LANES, (k + 1) * LANES) for k in range(ref.shape[-1] // LANES)]


def columns_kernel(*refs):
    grad_ref, part_ref = refs[10:]
    half = grad_ref.shape[2] // 2
    lists = grad_ref.shape[2] // LANES
    total = sum(ref[-EXTRA:][:1, :LANES] for ref in refs[:3])
    back = 1.0 / total

    def summed(m, k):
        if m == 1:
            own, low, high, far = (ref[:, k * LANES:(k + 1) * LANES] for ref in refs[6:10])
            return own + low + high + far
        piece, at = divmod(k * LANES, half)
        there = slice(at, at + LANES)
        kept, got, last = (ref[:ROWS, there] for ref in refs[3 * piece:3 * piece + 3])
        return kept + got + last

    for m in range(2):
        for k, cols in enumerate(chunks(grad_ref)):
            grad = summed(m, k) * back
            grad_ref[m, :, cols] = grad
            row = jnp.sum(grad * grad, axis=0, keepdims=True)
            part_ref[:, m * lists + k, :] = jnp.broadcast_to(row, (part_ref.shape[0], LANES))


def diagonal(n):
    shape = (n, n)
    return lax.broadcasted_iota(jnp.int32, shape, 0) == lax.broadcasted_iota(jnp.int32, shape, 1)


def to_row(column):
    return jnp.sum(jnp.where(diagonal(column.shape[0]), column, 0.0), axis=0, keepdims=True)


def to_column(row):
    return jnp.sum(jnp.where(diagonal(row.shape[1]), row, 0.0), axis=1, keepdims=True)


def rows_kernel(rows_all, part_ref, grad_ref, state_ref, weights_ref, cols_ref, out_ref):
    lists = grad_ref.shape[2] // LANES
    summed = jnp.sum(part_ref[...], axis=0)
    over, square, weight = [], [], []
    lane = lax.broadcasted_iota(jnp.int32, (1, LANES), 1)
    for m in range(2):
        zero = jnp.zeros((ROWS, LANES), jnp.float32)
        acc_over, acc_square, acc_weight = zero, zero, zero
        for k, cols in enumerate(chunks(grad_ref)):
            mean = summed[m * lists + k:m * lists + k + 1] * (1.0 / rows_all) + TINY
            new = DECAY * state_ref[m:m + 1, cols] + (1.0 - DECAY) * mean
            cols_ref[m:m + 1, cols] = new
            grad = grad_ref[m, :, cols]
            acc_square += grad * grad
            acc_over += grad * grad * (1.0 / new)
            w = weights_ref[m, :, cols]
            acc_weight += w * w
        over.append(jnp.sum(acc_over, axis=1, keepdims=True))
        square.append(jnp.sum(acc_square, axis=1, keepdims=True))
        both = jnp.sum(jnp.sum(acc_weight, axis=0, keepdims=True), axis=1, keepdims=True)
        weight.append(jnp.where(lane == m * ROWS, both, 0.0))
    lines = [to_row(jnp.concatenate(over, axis=0)), to_row(jnp.concatenate(square, axis=0))]
    lines.append(weight[0] + weight[1])
    for k in range(out_ref.shape[1]):
        line = lines[k] if k < len(lines) else jnp.zeros((1, LANES), jnp.float32)
        out_ref[:, k, :] = jnp.broadcast_to(line, (out_ref.shape[0], LANES))


def totals_kernel(cols_all, part_ref, state_ref, rows_ref, out_ref):
    summed = jnp.sum(part_ref[...], axis=0)
    state = to_row(jnp.concatenate([to_column(state_ref[m:m + 1]) for m in range(2)], axis=0))
    new = DECAY * state + (1.0 - DECAY) * (summed[1:2] * (1.0 / cols_all) + TINY)
    rows_ref[...] = new
    lane = lax.broadcasted_iota(jnp.int32, (1, LANES), 1)
    line = jnp.zeros((1, LANES), jnp.float32)
    for k, values in enumerate((summed[0:1] / new, new, summed[2:3])):
        for m in range(2):
            mine = (lane >= m * ROWS) & (lane < (m + 1) * ROWS)
            one = jnp.sum(jnp.where(mine, values, 0.0), axis=1, keepdims=True)
            line = jnp.where(lane == 2 * k + m, one, line)
    out_ref[...] = jnp.broadcast_to(line, out_ref.shape)


def update_kernel(rows_all, elements, *refs):
    part_ref, rows_ref, cols_ref, grad_ref, weights_ref = refs[:5]
    update_ref, new_ref, rows_out_ref, cols_out_ref = refs[5:]
    cols_out_ref[...] = cols_ref[...]
    summed = jnp.sum(part_ref[...], axis=0, keepdims=True)
    rows = to_column(rows_ref[...])
    for m in range(2):
        rows_out_ref[m:m + 1, :] = rows_ref[:, m * ROWS:(m + 1) * ROWS]
        ratio, rows_tot, weight = (summed[:, 2 * k + m:2 * k + m + 1] for k in range(3))
        mean_rows = rows_tot * (1.0 / rows_all)
        u_rms = jnp.sqrt(ratio * mean_rows * (1.0 / elements))
        w_rms = jnp.sqrt(weight * (1.0 / elements))
        factor = w_rms / jnp.maximum(1.0, u_rms)
        inverse = 1.0 / mean_rows
        here = rows[m * ROWS:(m + 1) * ROWS]
        for cols in chunks(grad_ref):
            second = here * cols_ref[m:m + 1, cols] * inverse
            step = grad_ref[m, :, cols] * lax.rsqrt(second) * factor
            update_ref[m, :, cols] = step
            new_ref[m, :, cols] = weights_ref[m, :, cols] - RATE * step


def pairing(first, kind):
    pairs = []
    for y in range(SIDE):
        for x in range(SIDE):
            for core in range(2):
                along_x = (core == 0) == first
                i = x if along_x else y
                j = (i ^ 1, SIDE - 1 - i, (i + 2) % SIDE)[kind]
                ny, nx = (y, j) if along_x else (j, x)
                pairs.append(((y * SIDE + x) * 2 + core, (ny * SIDE + nx) * 2 + core))
    return pairs


CORES = [(i, i ^ 1) for i in range(2 * SIDE * SIDE)]
PARTS = (((0, 2), (1, 3)), ((0, 1), (2, 3)))


def after(x, *earlier):
    return lax.optimization_barrier((x, *earlier))[0]


def body(activations, output_grads, token_counts, weights, row_state, col_state):
    ff_dev = output_grads.shape[2]
    rows_all = activations.shape[1]
    cols_all = ff_dev * lax.axis_size("mp")
    turned, first_grads = turn(activations, output_grads)
    tokens = activations.shape[0]
    half = ff_dev // 2
    quarter = SIDE * ROWS
    turned = turned.reshape(2, SIDE, quarter, tokens)

    def message(rows, i):
        return jax.ShapeDtypeStruct((rows + (EXTRA if i == 0 else 0), half), jnp.float32)

    pieces = 4
    got = [None] * pieces
    sent = [None] * pieces
    kept = [None] * pieces
    out = [None] * pieces

    grads = [first_grads, None]

    def swap(i, *earlier):
        if i == 1:
            out[1], grads[1] = pl.pallas_call(
                first_kernel,
                out_shape=(message(SIDE * quarter, 1), jax.ShapeDtypeStruct(first_grads.shape, first_grads.dtype)),
                in_specs=[VMEM, VMEM, VMEM, FAR],
                out_specs=(VMEM, VMEM),
                scratch_shapes=[pltpu.SemaphoreType.DMA],
                cost_estimate=pl.CostEstimate(flops=0, bytes_accessed=0, transcendentals=0),
                compiler_params=pltpu.CompilerParams(vmem_limit_bytes=FIRST_LIMIT),
            )(after(turned, *earlier), token_counts, first_grads, output_grads)
        else:
            kernel = functools.partial(theirs_kernel, i % 2)
            out[i] = call(kernel, message(SIDE * quarter, i), [VMEM] * 3)(
                after(turned, *earlier), token_counts, grads[i // 2]
            )
        got[i] = lax.ppermute(out[i], "dp", CORES)

    def share_of(i, which, came, *earlier):
        kernel = functools.partial(mine_kernel, i % 2, which)
        return call(kernel, message(2 * quarter, i), [VMEM] * 4)(
            after(turned, *earlier), token_counts, grads[i // 2], came
        )

    swapped = [None] * pieces

    def first(i, *earlier):
        swapped[i] = got[i]
        sent[i] = share_of(i, 1, swapped[i], *earlier)
        got[i] = lax.ppermute(sent[i], "dp", pairing(True, i % 2))

    swap(0)
    for i in range(1, pieces):
        swap(i, out[i - 1])
    first(0, out[3])
    for i in range(1, pieces):
        first(i, sent[i - 1])
    last = sent[3]
    for i in range(pieces):
        last = kept[i] = share_of(i, 0, swapped[i], last)
    final = [None] * pieces
    for i in range(pieces):
        kernel = functools.partial(onward_kernel, quarter)
        last = call(kernel, message(quarter, i), [VMEM] * 2)(kept[i], after(got[i], last))
        final[i] = lax.ppermute(last, "dp", pairing(True, 1 - i % 2))
    share = jax.ShapeDtypeStruct((ROWS, ff_dev), jnp.float32)

    def deal(m):
        nonlocal last
        terms = [t for i in (2 * m, 2 * m + 1) for t in (kept[i], got[i], final[i])]
        terms[0] = after(terms[0], last)
        own, low, high, far = call(deal_kernel, (share,) * 4, [VMEM] * 6)(*terms)
        last = own
        low = lax.ppermute(low, "dp", pairing(False, 0))
        high = lax.ppermute(high, "dp", pairing(False, 1))
        far = lax.ppermute(far, "dp", pairing(False, 2))
        return own, low, high, far

    held = []
    for i in range(2):
        kernel = functools.partial(across_kernel, i)
        last, keep = call(kernel, (message(2 * ROWS, i),) * 2, [VMEM] * 3)(
            kept[i], got[i], after(final[i], last)
        )
        held.append([keep, lax.ppermute(last, "dp", pairing(False, i % 2))])
    for i in (0,):
        keep, came = held[i]
        kernel = functools.partial(onward_kernel, ROWS)
        last = call(kernel, message(ROWS, i), [VMEM] * 2)(keep, after(came, last))
        held[i].append(lax.ppermute(last, "dp", pairing(False, 1 - i % 2)))
    dealt = deal(1)
    for i in (1,):
        keep, came = held[i]
        kernel = functools.partial(onward_kernel, ROWS)
        last = call(kernel, message(ROWS, i), [VMEM] * 2)(keep, after(came, last))
        held[i].append(lax.ppermute(last, "dp", pairing(False, 1 - i % 2)))
    f32 = jnp.float32
    mine_shape = jax.ShapeDtypeStruct((2, ROWS, ff_dev), f32)
    lists = 2 * ff_dev // LANES
    dp_n, mp_n = lax.axis_size("dp"), lax.axis_size("mp")
    grad, part = call(
        columns_kernel,
        (mine_shape, jax.ShapeDtypeStruct((dp_n, lists, LANES), f32)),
        [VMEM] * 10,
    )(*held[0], *held[1], *dealt)
    part = lax.all_to_all(part, "dp", 0, 0, tiled=True)
    line = jax.ShapeDtypeStruct((1, LANES), f32)
    cols_new, part = call(
        functools.partial(rows_kernel, rows_all),
        (jax.ShapeDtypeStruct((2, ff_dev), f32), jax.ShapeDtypeStruct((mp_n, 4, LANES), f32)),
        [VMEM] * 4,
    )(part, grad, col_state, weights)
    part = lax.all_to_all(part, "mp", 0, 0, tiled=True)
    rows_new, part = call(
        functools.partial(totals_kernel, cols_all),
        (jax.ShapeDtypeStruct((1, LANES), f32), jax.ShapeDtypeStruct((dp_n, LANES), f32)),
        [VMEM] * 2,
    )(part, row_state)
    part = lax.all_to_all(part, "dp", 0, 0, tiled=True)
    rows_shape, cols_shape = (jax.ShapeDtypeStruct(t.shape, f32) for t in (row_state, col_state))
    return call(
        functools.partial(update_kernel, rows_all, rows_all * cols_all),
        (mine_shape, mine_shape, rows_shape, cols_shape),
        [VMEM] * 5,
    )(part, rows_new, cols_new, grad, weights)


def solution(mesh):
    in_specs = (
        P("dp", None),
        P(None, "dp", "mp"),
        P("dp", None),
        P(None, "dp", "mp"),
        P(None, "dp"),
        P(None, "mp"),
    )
    out_specs = (P(None, "dp", "mp"), P(None, "dp", "mp"), P(None, "dp"), P(None, "mp"))
    return jax.shard_map(body, mesh=mesh, in_specs=in_specs, out_specs=out_specs, check_vma=False)
```
